32 devices in a mesh: seq: 8 (over z, y), fsdp: 4 (over x, core).
Axes of the slice: x: 2, y: 2, z: 4, core: 2. Of those that a mesh axis runs over, the one named last changes fastest.
Arguments:
- tokens: bfloat16 [8, 4096, 768], P('fsdp', 'seq'), may hold values from -6 to 6
- norm_gain_attn: bfloat16 [768], P('fsdp'), may hold values from 0.5 to 1.5
- qkv_weight: bfloat16 [768, 2304], P('fsdp'), may hold values from -0.21875 to 0.21875
- attn_out_weight: bfloat16 [768, 768], P('fsdp'), may hold values from -2.5 to 2.5
- norm_gain_mlp: bfloat16 [768], P('fsdp'), may hold values from 0.5 to 1.5
- mlp_in_weight: bfloat16 [768, 2304], P('fsdp'), may hold values from -0.21875 to 0.21875
- mlp_out_weight: bfloat16 [1152, 768], P('fsdp'), may hold values from -0.1875 to 0.1875
- grad_out: bfloat16 [8, 4096, 768], P('fsdp', 'seq'), may hold values from -16 to 16
Outputs:
- block_out: bfloat16 [8, 4096, 768], P('fsdp', 'seq')
- tokens_grad: float32 [8, 4096, 768], P('fsdp', 'seq')
- norm_gain_attn_grad: float32 [768], P('fsdp')
- qkv_weight_grad: float32 [768, 2304], P('fsdp')
- attn_out_weight_grad: float32 [768, 768], P('fsdp')
- norm_gain_mlp_grad: float32 [768], P('fsdp')
- mlp_in_weight_grad: float32 [768, 2304], P('fsdp')
- mlp_out_weight_grad: float32 [1152, 768], P('fsdp')
The draws below stay inside these ranges and needn't reach their ends.
All inputs are finite; a program needn't handle non-finite values.
Results may differ from the reference program's by a relative error of at most 0.018.
Values may be sent and summed in bfloat16 or wider, within the bound.
A program may use at most 256 MiB of HBM per device.

```python
import math
import jax
import jax.numpy as jnp
from jax import lax

D = 768
HEADS = 12
HEAD_DIM = 64
FF = 1152
WIN = 64
PIECE = 512
SEQS = 8
LEN = 4096


def draw_grad_out(key, part):
    key = jax.random.fold_in(key, 7)
    placing = jnp.arange(LEN, dtype=jnp.float32) / LEN
    raw_values = jnp.clip(jax.random.normal(key, (SEQS, LEN, D), jnp.float32), -4.0, 4.0)
    rising = jnp.exp(jnp.log(3.0) * placing)
    return (raw_values * rising[None, :, None]).astype(jnp.bfloat16)


def levels(key, dims, cuts, least, top_value):
    def one(position, parts):
        draws = jax.random.uniform(jax.random.fold_in(jax.random.fold_in(key, 6), position), (parts,), jnp.float32, least / len(cuts), top_value / len(cuts))
        return jnp.repeat(jnp.exp(draws), dims[position] // parts).reshape((-1,) + (1,) * (len(dims) - position - 1))

    gain = one(*cuts[0])
    for cut in cuts[1:]:
        gain = gain * one(*cut)
    return gain


def normal_values(key, shape, deviation, bound, pieces=(), kind=jnp.bfloat16):
    drawn = deviation * jax.random.normal(key, shape, jnp.float32)
    if pieces:
        drawn = drawn * levels(key, shape, pieces, -0.22, 0.18)
    return jnp.clip(drawn, -bound, bound).astype(kind)


def setup_inputs(seed: int = 0) -> dict:
    arg_keys = jax.random.split(jax.random.key(seed), 9)
    tokens = normal_values(arg_keys[0], (SEQS, LEN, D), 1.0, 6.0, ((0, 4), (1, 8)))
    norm_gain_attn = jnp.clip(1.0 + 0.1 * jax.random.normal(arg_keys[1], (D,), jnp.float32), 0.5, 1.5).astype(jnp.bfloat16)
    qkv_weight = normal_values(arg_keys[2], (D, 3 * D), D ** -0.5, 0.21875, ((0, 4),))
    attn_out_weight = normal_values(arg_keys[3], (D, D), (max(D // (2 * WIN + 1), 1)) ** -0.5, 2.5, ((0, 4),))
    norm_gain_mlp = jnp.clip(1.0 + 0.1 * jax.random.normal(arg_keys[4], (D,), jnp.float32), 0.5, 1.5).astype(jnp.bfloat16)
    mlp_in_weight = normal_values(arg_keys[5], (D, 2 * FF), D ** -0.5, 0.21875, ((0, 4),))
    mlp_out_weight = normal_values(arg_keys[6], (FF, D), FF ** -0.5, 0.1875, ((0, 4),))
    grad_out = draw_grad_out(jax.random.fold_in(arg_keys[8], 71), 0)
    return dict(tokens=tokens, norm_gain_attn=norm_gain_attn, qkv_weight=qkv_weight, attn_out_weight=attn_out_weight, norm_gain_mlp=norm_gain_mlp, mlp_in_weight=mlp_in_weight, mlp_out_weight=mlp_out_weight, grad_out=grad_out)


epsilon = 1e-05
rope_base = 10000.0
negative = -1e+30

@jax.custom_vjp
def low(v):
    return lax.optimization_barrier(v.astype(jnp.bfloat16)).astype(jnp.float32)

@jax.custom_vjp
def low_back(v):
    return v

def low_keep(v):
    return (low(v), None)

def low_pass(kept, grad):
    return (grad,)

def back_keep(v):
    return (v, None)

def back_low(kept, grad):
    return (low(grad),)
low.defvjp(low_keep, low_pass)
low_back.defvjp(back_keep, back_low)

def layer_norm(values, gain_row):
    center = values - lax.optimization_barrier(jnp.mean(values, axis=-1, keepdims=True))
    spread = lax.optimization_barrier(jnp.mean(center * center, axis=-1, keepdims=True))
    return center * lax.rsqrt(spread + epsilon) * gain_row

def rope_tables(positions):
    half_dim = HEAD_DIM // 2
    freqs = rope_base ** (-(jnp.arange(half_dim, dtype=jnp.float32) * 2.0 / HEAD_DIM))
    angles = positions[:, None] * freqs[None, :]
    angles = jnp.concatenate([angles, angles], axis=-1)
    return (jnp.cos(angles), jnp.sin(angles))

def rotate(values, cosine, sine):
    half_dim = HEAD_DIM // 2
    turned = jnp.concatenate([-values[..., half_dim:], values[..., :half_dim]], axis=-1)
    return values * cosine[:, None, :] + turned * sine[:, None, :]

def attend(query, key_rows, value_rows):
    score_scale = 1.0 / math.sqrt(HEAD_DIM)
    key_span = PIECE + 2 * WIN
    padding = jnp.zeros((WIN, HEADS, HEAD_DIM), jnp.float32)
    key_padded = jnp.concatenate([padding, key_rows, padding], axis=0)
    value_padded = jnp.concatenate([padding, value_rows, padding], axis=0)

    def one_block(offset):
        query_block = lax.dynamic_slice_in_dim(query, offset, PIECE, 0)
        key_block = lax.dynamic_slice_in_dim(key_padded, offset, key_span, 0)
        value_block = lax.dynamic_slice_in_dim(value_padded, offset, key_span, 0)
        scores = jnp.einsum('qhd,khd->hqk', query_block, key_block, precision=lax.Precision.HIGHEST) * score_scale
        scores = low_back(scores)
        query_pos = offset + jnp.arange(PIECE, dtype=jnp.int32)
        key_pos = offset - WIN + jnp.arange(key_span, dtype=jnp.int32)
        inside = (jnp.abs(query_pos[:, None] - key_pos[None, :]) <= WIN) & (key_pos[None, :] >= 0) & (key_pos[None, :] < LEN)
        scores = jnp.where(inside[None], scores, negative)
        highest = lax.optimization_barrier(jnp.max(scores, axis=-1, keepdims=True))
        raised = jnp.exp(scores - highest)
        weights = low(raised / lax.optimization_barrier(jnp.sum(raised, axis=-1, keepdims=True)))
        return jnp.einsum('hqk,khd->qhd', weights, value_block, precision=lax.Precision.HIGHEST)
    offsets = jnp.arange(LEN // PIECE, dtype=jnp.int32) * PIECE
    blocks = lax.map(jax.checkpoint(one_block), offsets)
    return blocks.reshape(LEN, HEADS * HEAD_DIM)

def forward(inputs, gain_attn, weight_qkv, weight_attn, gain_mlp, weight_in, weight_out):
    normed = low(layer_norm(inputs, gain_attn))
    projected = low_back(jnp.dot(normed, weight_qkv, precision=lax.Precision.HIGHEST))
    projected = projected.reshape(LEN, 3, HEADS, HEAD_DIM)
    cosine, sine = rope_tables(jnp.arange(LEN, dtype=jnp.int32).astype(jnp.float32))
    query = low(rotate(projected[:, 0], cosine, sine))
    key_rows = low(rotate(projected[:, 1], cosine, sine))
    value_rows = low(projected[:, 2])
    attended = low(low_back(attend(query, key_rows, value_rows)))
    middle = inputs + low_back(jnp.dot(attended, weight_attn, precision=lax.Precision.HIGHEST))
    normed_mlp = low(layer_norm(middle, gain_mlp))
    widened = low_back(jnp.dot(normed_mlp, weight_in, precision=lax.Precision.HIGHEST))
    hidden = low(jax.nn.gelu(widened[:, :FF], approximate=False) * widened[:, FF:])
    return middle + low_back(jnp.dot(hidden, weight_out, precision=lax.Precision.HIGHEST))

def reference(tokens, norm_gain_attn, qkv_weight, attn_out_weight, norm_gain_mlp, mlp_in_weight, mlp_out_weight, grad_out):
    params = (norm_gain_attn.astype(jnp.float32), qkv_weight.astype(jnp.float32), attn_out_weight.astype(jnp.float32), norm_gain_mlp.astype(jnp.float32), mlp_in_weight.astype(jnp.float32), mlp_out_weight.astype(jnp.float32))

    def per_sequence(running, sequence_pair):
        inputs, cotangent = sequence_pair
        output, pullback = jax.vjp(forward, inputs.astype(jnp.float32), *params)
        gradients = pullback(cotangent.astype(jnp.float32))
        running = tuple((kept_sum + addend for kept_sum, addend in zip(running, gradients[1:])))
        return (running, (output.astype(jnp.bfloat16), gradients[0]))
    starting = tuple((jnp.zeros(parameter.shape, jnp.float32) for parameter in params))
    totals, (outputs, input_grads) = lax.scan(per_sequence, starting, (tokens, grad_out))
    return (outputs, input_grads, totals[0], totals[1], totals[2], totals[3], totals[4], totals[5])
```

```python
import math

import jax
import jax.numpy as jnp
from jax import lax
from jax.experimental import pallas as pl
from jax.experimental.pallas import tpu as pltpu
from jax.sharding import PartitionSpec as P

HEADS = 12
HEAD_DIM = 64
FF = 1152
WIN = 64
PAIR = 128
BLOCK = 128

epsilon = 1e-05
rope_base = 10000.0
negative = -1e30
f32 = jnp.float32
bf16 = jnp.bfloat16
LIMIT = 56 * 1024 * 1024

NN = (((1,), (0,)), ((), ()))
NT = (((1,), (1,)), ((), ()))
TN = (((0,), (0,)), ((), ()))


def mm(a, b, dims=NN):
    return lax.dot_general(a, b, dims, preferred_element_type=f32)


def unit_rows(x):
    center = x - jnp.mean(x, axis=-1, keepdims=True)
    inverse = lax.rsqrt(jnp.mean(center * center, axis=-1, keepdims=True) + epsilon)
    return center * inverse, inverse


def turn(x, cos, low, high):
    return x * cos + pltpu.roll(x, PAIR - 32, 1) * low + pltpu.roll(x, 32, 1) * high


def qkv_kernel(tok_ref, gain_ref, w_ref, cos_ref, low_ref, high_ref, q_ref, kv_ref):
    unit, _ = unit_rows(tok_ref[...].astype(f32))
    normed = (unit * gain_ref[...]).astype(bf16)
    cos, low, high = cos_ref[...], low_ref[...], high_ref[...]
    width = q_ref.shape[1]
    step = 2 * PAIR
    for j in range(3 * width // step):
        part = mm(normed, w_ref[:, j * step : (j + 1) * step])
        for h in range(2):
            at = j * step + h * PAIR
            piece = part[:, h * PAIR : (h + 1) * PAIR]
            if at < width:
                q_ref[:, at : at + PAIR] = (
                    turn(piece, cos, low, high) * (1.0 / math.sqrt(HEAD_DIM))
                ).astype(bf16)
            elif at < 2 * width:
                kv_ref[:, at - width : at - width + PAIR] = turn(piece, cos, low, high).astype(bf16)
            else:
                kv_ref[:, at - width : at - width + PAIR] = piece.astype(bf16)


def head_masks():
    lane = lax.broadcasted_iota(jnp.int32, (1, PAIR), 1)
    first = (lane < HEAD_DIM).astype(f32)
    return first.astype(bf16), (1.0 - first).astype(bf16), lane < HEAD_DIM


def fill(dst, left, mid, right):
    n = mid.shape[1]
    dst[0:WIN] = left[0]
    dst[WIN : WIN + n] = mid[0]
    dst[WIN + n : 2 * WIN + n] = right[0]


def attend_kernel(q_ref, k_ref, v_ref, lk_ref, lv_ref, rk_ref, rv_ref, bias_ref, att_ref, p_ref, ke, ve):
    fill(ke, lk_ref, k_ref, rk_ref)
    fill(ve, lv_ref, v_ref, rv_ref)
    first, second, is_first = head_masks()
    for i in range(q_ref.shape[1] // BLOCK):
        rows = slice(i * BLOCK, (i + 1) * BLOCK)
        span = slice(i * BLOCK, (i + 1) * BLOCK + 2 * WIN)
        query, key, value = q_ref[0, rows], ke[span], ve[span]
        outs = []
        for h, mask in enumerate((first, second)):
            scores = mm(query * mask, key, NT) + bias_ref[i]
            raised = jnp.exp(scores - jnp.max(scores, axis=-1, keepdims=True))
            total = jnp.sum(raised, axis=-1, keepdims=True)
            probs = (raised * (1.0 / total)).astype(bf16)
            p_ref[0, h, rows] = probs
            outs.append(mm(probs, value))
        att_ref[0, rows] = jnp.where(is_first, outs[0], outs[1]).astype(bf16)


def attend_back_kernel(
    q_ref, k_ref, v_ref, lk_ref, lv_ref, rk_ref, rv_ref, p_ref, ag_ref, cos_ref, low_ref, high_ref,
    dq_ref, dk_ref, dv_ref, dl_ref, dr_ref, ke, ve, ka, va,
):
    fill(ke, lk_ref, k_ref, rk_ref)
    fill(ve, lv_ref, v_ref, rv_ref)
    ka[...] = jnp.zeros_like(ka)
    va[...] = jnp.zeros_like(va)
    first, second, is_first = head_masks()
    count = q_ref.shape[1]
    scale = 1.0 / math.sqrt(HEAD_DIM)
    for i in range(count // BLOCK):
        rows = slice(i * BLOCK, (i + 1) * BLOCK)
        span = slice(i * BLOCK, (i + 1) * BLOCK + 2 * WIN)
        query, key, value, upstream = q_ref[0, rows], ke[span], ve[span], ag_ref[0, rows]
        dqs, dks, dvs = [], [], []
        for h, mask in enumerate((first, second)):
            low_probs = p_ref[0, h, rows]
            probs = low_probs.astype(f32)
            back = mm(upstream * mask, value, NT)
            weighted = probs * back
            delta = jnp.sum(weighted, axis=-1, keepdims=True)
            grad = (weighted - probs * delta).astype(bf16)
            dqs.append(mm(grad, key))
            dks.append(mm(grad, query, TN))
            dvs.append(mm(low_probs, upstream, TN))
        dq = jnp.where(is_first, dqs[0], dqs[1]) * scale
        at = slice(WIN + i * BLOCK, WIN + (i + 1) * BLOCK)
        dq_ref[0, rows] = turn(dq, cos_ref[at], -low_ref[at], -high_ref[at]).astype(bf16)
        ka[span] += jnp.where(is_first, dks[0], dks[1])
        va[span] += jnp.where(is_first, dvs[0], dvs[1])
    dk = turn(ka[...], cos_ref[...], -low_ref[...], -high_ref[...])
    dl_ref[0, 0] = dk[:WIN].astype(bf16)
    dk_ref[0] = dk[WIN : WIN + count].astype(bf16)
    dr_ref[0, 0] = dk[WIN + count :].astype(bf16)
    dl_ref[0, 1] = va[:WIN].astype(bf16)
    dv_ref[0] = va[WIN : WIN + count].astype(bf16)
    dr_ref[0, 1] = va[WIN + count :].astype(bf16)


def mlp_kernel(
    tok_ref, att_ref, go_ref, gain_ref, wo_ref, win_ref, wout_ref,
    out_ref, mg_ref, ag_ref, dwo_ref, dwin_ref, dwout_ref, dgain_ref,
    awo, awin, awout, wg_buf, hid_buf,
):
    step = pl.program_id(0)

    @pl.when(step == 0)
    def _():
        awo[...] = jnp.zeros_like(awo)
        awin[...] = jnp.zeros_like(awin)
        awout[...] = jnp.zeros_like(awout)
        dgain_ref[...] = jnp.zeros_like(dgain_ref)

    attended, go = att_ref[...], go_ref[...]
    middle = tok_ref[...].astype(f32) + mm(attended, wo_ref[...])
    gain = gain_ref[...]
    unit, inverse = unit_rows(middle)
    normed = (unit * gain).astype(bf16)
    chunk = 384
    for c in range(FF // chunk):
        cols = slice(c * chunk, (c + 1) * chunk)
        gate = slice(FF + c * chunk, FF + (c + 1) * chunk)
        a = mm(normed, win_ref[:, cols])
        b = mm(normed, win_ref[:, gate])
        hg = mm(go, wout_ref[cols, :], NT)
        cdf = 0.5 * (1.0 + lax.erf(a * (1.0 / math.sqrt(2.0))))
        gelu = a * cdf
        slope = cdf + a * (jnp.exp(-0.5 * a * a) * (1.0 / math.sqrt(2.0 * math.pi)))
        hid_buf[:, cols] = (gelu * b).astype(bf16)
        wg_buf[:, cols] = (hg * b * slope).astype(bf16)
        wg_buf[:, gate] = (hg * gelu).astype(bf16)
    hidden, wg = hid_buf[...], wg_buf[...]
    out_ref[...] = (middle + mm(hidden, wout_ref[...])).astype(bf16)
    back = mm(wg, win_ref[...], NT)
    dgain_ref[...] += jnp.sum(back * unit, axis=0, keepdims=True)
    e = back * gain
    part = e - jnp.mean(e, axis=-1, keepdims=True) - unit * jnp.mean(e * unit, axis=-1, keepdims=True)
    mg = go.astype(f32) + inverse * part
    mg_ref[...] = mg
    low = mg.astype(bf16)
    ag_ref[...] = mm(low, wo_ref[...], NT).astype(bf16)
    awout[...] += mm(hidden, go, TN)
    awin[...] += mm(normed, wg, TN)
    awo[...] += mm(attended, low, TN)

    @pl.when(step == pl.num_programs(0) - 1)
    def _():
        dwo_ref[...] = awo[...].astype(bf16)
        dwin_ref[...] = awin[...].astype(bf16)
        dwout_ref[...] = awout[...].astype(bf16)


def qkv_back_kernel(
    tok_ref, mg_ref, dq_ref, dk_ref, dv_ref, fl_ref, fr_ref, gain_ref, w_ref,
    tg_ref, dw_ref, dgain_ref, acc, buf,
):
    step = pl.program_id(0)

    @pl.when(step == 0)
    def _():
        acc[...] = jnp.zeros_like(acc)
        dgain_ref[...] = jnp.zeros_like(dgain_ref)

    width = tok_ref.shape[2]
    count = tok_ref.shape[1]
    buf[:, :width] = dq_ref[0]
    for j, ref in enumerate((dk_ref, dv_ref)):
        cols = slice((j + 1) * width, (j + 2) * width)
        buf[:, cols] = ref[0]
        buf[:WIN, cols] = (ref[0, :WIN].astype(f32) + fl_ref[0, j].astype(f32)).astype(bf16)
        buf[count - WIN :, cols] = (
            ref[0, count - WIN :].astype(f32) + fr_ref[0, j].astype(f32)
        ).astype(bf16)
    gain = gain_ref[...]
    unit, inverse = unit_rows(tok_ref[0].astype(f32))
    normed = (unit * gain).astype(bf16)
    grads = buf[...]
    back = mm(grads, w_ref[...], NT)
    dgain_ref[...] += jnp.sum(back * unit, axis=0, keepdims=True)
    e = back * gain
    part = e - jnp.mean(e, axis=-1, keepdims=True) - unit * jnp.mean(e * unit, axis=-1, keepdims=True)
    tg_ref[0] = mg_ref[0] + inverse * part
    acc[...] += mm(normed, grads, TN)

    @pl.when(step == pl.num_programs(0) - 1)
    def _():
        dw_ref[...] = acc[...].astype(bf16)


def sds(shape, dtype):
    return jax.ShapeDtypeStruct(shape, dtype)


def whole(shape):
    return pl.BlockSpec(shape, lambda *_: (0,) * len(shape), pipeline_mode=pl.Buffered(1))


def tables(start, count):
    half = HEAD_DIM // 2
    freqs = rope_base ** (-(jnp.arange(half, dtype=f32) * 2.0 / HEAD_DIM))
    positions = (start + jnp.arange(count, dtype=jnp.int32)).astype(f32)
    angles = positions[:, None] * freqs[None, :]
    cos, sin = jnp.cos(angles), jnp.sin(angles)
    none = jnp.zeros_like(sin)
    return (
        jnp.concatenate([cos] * 4, axis=-1),
        jnp.concatenate([-sin, none] * 2, axis=-1),
        jnp.concatenate([none, sin] * 2, axis=-1),
    )


def shards(tokens, norm_gain_attn, qkv_weight, attn_out_weight, norm_gain_mlp, mlp_in_weight, mlp_out_weight, grad_out):
    seqs, piece, width = tokens.shape
    rows = seqs * piece
    span = piece + 2 * WIN
    pairs = width // PAIR
    seq_size = lax.axis_size("seq")
    forward = [(i, i + 1) for i in range(seq_size - 1)]
    backward = [(j, i) for i, j in forward]
    gather = lambda x: lax.all_gather(x, "fsdp", axis=0, tiled=True)
    w_qkv = gather(qkv_weight)
    gains = lax.all_gather(jnp.stack([norm_gain_attn, norm_gain_mlp]), "fsdp", axis=1, tiled=True)
    w_attn = gather(attn_out_weight)
    w_in = gather(mlp_in_weight)
    w_out = gather(mlp_out_weight)
    gain_attn = gains[0:1].astype(f32)
    gain_mlp = gains[1:2].astype(f32)
    start = lax.axis_index("seq") * piece
    cos, low, high = tables(start - WIN, span)
    q_at = start + jnp.arange(piece, dtype=jnp.int32).reshape(-1, BLOCK)[:, :, None]
    k_at = (
        start - WIN
        + jnp.arange(piece // BLOCK, dtype=jnp.int32)[:, None, None] * BLOCK
        + jnp.arange(BLOCK + 2 * WIN, dtype=jnp.int32)[None, None, :]
    )
    inside = (jnp.abs(q_at - k_at) <= WIN) & (k_at >= 0) & (k_at < piece * seq_size)
    bias = jnp.where(inside, 0.0, negative).astype(f32)

    tile = 256
    per = piece // tile
    flat = lambda x: x.reshape(rows, x.shape[-1])
    row_spec = lambda w: pl.BlockSpec((tile, w), lambda i: (i, 0))
    table_spec = pl.BlockSpec((tile, PAIR), lambda i: (lax.rem(i, per), 0))
    params = lambda n: pltpu.CompilerParams(dimension_semantics=("arbitrary",) * n, vmem_limit_bytes=LIMIT)
    tok = flat(tokens)
    mid = slice(WIN, WIN + piece)
    q, kv = pl.pallas_call(
        qkv_kernel,
        grid=(rows // tile,),
        in_specs=[row_spec(width), whole((1, width)), whole(w_qkv.shape), table_spec, table_spec, table_spec],
        out_specs=[row_spec(width), row_spec(2 * width)],
        out_shape=[sds((rows, width), bf16), sds((rows, 2 * width), bf16)],
        compiler_params=params(1),
        cost_estimate=pl.CostEstimate(flops=6 * rows * width * width, bytes_accessed=12 * rows * width, transcendentals=0),
        name="qkv_forward",
    )(tok, gain_attn, w_qkv, cos[mid], low[mid], high[mid])
    q = q.reshape(seqs, piece, width)
    kv = kv.reshape(seqs, piece, 2 * width)
    left = lax.ppermute(kv[:, piece - WIN :], "seq", forward)
    right = lax.ppermute(kv[:, :WIN], "seq", backward)

    def lanes(n, off=0):
        return pl.BlockSpec((1, n, PAIR), lambda s, p: (s, 0, p + off))

    kv_specs = [
        lanes(piece), lanes(piece, pairs), lanes(WIN), lanes(WIN, pairs), lanes(WIN), lanes(WIN, pairs),
    ]
    kv_args = (kv, kv, left, left, right, right)
    p_spec = pl.BlockSpec((1, 2, piece, BLOCK + 2 * WIN), lambda s, p: (s, p, 0, 0))
    p_shape = (seqs, HEADS, piece, BLOCK + 2 * WIN)
    ext = pltpu.VMEM((span, PAIR), bf16)
    unit_flops = 2 * seqs * HEADS * piece * (BLOCK + 2 * WIN) * HEAD_DIM
    p_bytes = 2 * math.prod(p_shape)
    attended, probs = pl.pallas_call(
        attend_kernel,
        grid=(seqs, pairs),
        in_specs=[lanes(piece)] + kv_specs + [whole(bias.shape)],
        out_specs=[lanes(piece), p_spec],
        out_shape=[sds((seqs, piece, width), bf16), sds(p_shape, bf16)],
        scratch_shapes=[ext, ext],
        compiler_params=params(2),
        cost_estimate=pl.CostEstimate(flops=8 * unit_flops, bytes_accessed=p_bytes + 8 * rows * width, transcendentals=p_bytes // 2),
        name="attend_forward",
    )(q, *kv_args, bias)

    out, mg, ag, d_wo, d_win, d_wout, d_gain_mlp = pl.pallas_call(
        mlp_kernel,
        grid=(rows // tile,),
        in_specs=[row_spec(width)] * 3 + [whole((1, width)), whole(w_attn.shape), whole(w_in.shape), whole(w_out.shape)],
        out_specs=[row_spec(width)] * 3
        + [whole(w_attn.shape), whole(w_in.shape), whole(w_out.shape), whole((1, width))],
        out_shape=[
            sds((rows, width), bf16), sds((rows, width), f32), sds((rows, width), bf16),
            sds(w_attn.shape, bf16), sds(w_in.shape, bf16), sds(w_out.shape, bf16), sds((1, width), f32),
        ],
        scratch_shapes=[
            pltpu.VMEM(w_attn.shape, f32), pltpu.VMEM(w_in.shape, f32), pltpu.VMEM(w_out.shape, f32),
            pltpu.VMEM((tile, 2 * FF), bf16), pltpu.VMEM((tile, FF), bf16),
        ],
        compiler_params=params(1),
        cost_estimate=pl.CostEstimate(flops=6 * rows * width * (width + 3 * FF), bytes_accessed=40 * 2**20, transcendentals=0),
        name="mlp_both_ways",
    )(tok, flat(attended), flat(grad_out), gain_mlp, w_attn, w_in, w_out)

    def reduce(x, dim=0):
        mine = lax.psum_scatter(x, "fsdp", scatter_dimension=dim, tiled=True)
        return mine

    s_win, s_wout, s_wo = reduce(d_win), reduce(d_wout), reduce(d_wo)
    s_win, s_wout, s_wo = lax.psum((s_win, s_wout, s_wo), "seq")

    table_full = pl.BlockSpec((span, PAIR), lambda s, p: (0, 0))
    edge = pl.BlockSpec((1, 2, WIN, PAIR), lambda s, p: (s, 0, 0, p))
    edge_shape = sds((seqs, 2, WIN, width), bf16)
    own = sds((seqs, piece, width), bf16)
    total = pltpu.VMEM((span, PAIR), f32)
    dq, dk, dv, dl, dr = pl.pallas_call(
        attend_back_kernel,
        grid=(seqs, pairs),
        in_specs=[lanes(piece)] + kv_specs + [p_spec, lanes(piece), table_full, table_full, table_full],
        out_specs=[lanes(piece)] * 3 + [edge, edge],
        out_shape=[own] * 3 + [edge_shape] * 2,
        scratch_shapes=[ext, ext, total, total],
        compiler_params=params(2),
        cost_estimate=pl.CostEstimate(flops=16 * unit_flops, bytes_accessed=p_bytes + 16 * rows * width, transcendentals=0),
        name="attend_backward",
    )(q, *kv_args, probs, ag.reshape(seqs, piece, width), cos, low, high)
    from_left = lax.ppermute(dr, "seq", forward)
    from_right = lax.ppermute(dl, "seq", backward)

    seq_spec = pl.BlockSpec((1, piece, width), lambda s: (s, 0, 0))
    edge_in = pl.BlockSpec((1, 2, WIN, width), lambda s: (s, 0, 0, 0))
    tokens_grad, d_wqkv, d_gain_attn = pl.pallas_call(
        qkv_back_kernel,
        grid=(seqs,),
        in_specs=[seq_spec] * 5 + [edge_in] * 2 + [whole((1, width)), whole(w_qkv.shape)],
        out_specs=[seq_spec, whole(w_qkv.shape), whole((1, width))],
        out_shape=[sds((seqs, piece, width), f32), sds(w_qkv.shape, bf16), sds((1, width), f32)],
        scratch_shapes=[pltpu.VMEM(w_qkv.shape, f32), pltpu.VMEM((piece, 3 * width), bf16)],
        compiler_params=params(1),
        cost_estimate=pl.CostEstimate(flops=12 * rows * width * width, bytes_accessed=20 * rows * width, transcendentals=0),
        name="qkv_backward",
    )(tokens, mg.reshape(seqs, piece, width), dq, dk, dv, from_left, from_right, gain_attn, w_qkv)

    s_gains = lax.psum_scatter(
        jnp.concatenate([d_gain_attn, d_gain_mlp]).astype(bf16), "fsdp", scatter_dimension=1, tiled=True
    ).astype(f32)
    s_wqkv = reduce(d_wqkv)
    s_gains, s_wqkv = lax.psum((s_gains, s_wqkv), "seq")
    return (
        out.reshape(seqs, piece, width),
        tokens_grad,
        s_gains[0],
        s_wqkv.astype(f32),
        s_wo.astype(f32),
        s_gains[1],
        s_win.astype(f32),
        s_wout.astype(f32),
    )


def solution(mesh):
    return jax.shard_map(
        shards,
        mesh=mesh,
        in_specs=(
            P("fsdp", "seq", None),
            P("fsdp"),
            P("fsdp", None),
            P("fsdp", None),
            P("fsdp"),
            P("fsdp", None),
            P("fsdp", None),
            P("fsdp", "seq", None),
        ),
        out_specs=(
            P("fsdp", "seq", None),
            P("fsdp", "seq", None),
            P("fsdp"),
            P("fsdp", None),
            P("fsdp", None),
            P("fsdp"),
            P("fsdp", None),
            P("fsdp", None),
        ),
        check_vma=False,
    )
```

```python
import math

import jax
import jax.numpy as jnp
from jax import lax
from jax.experimental import pallas as pl
from jax.experimental.pallas import tpu as pltpu
from jax.sharding import PartitionSpec as P

HEADS = 12
HEAD_DIM = 64
FF = 1152
WIN = 64
PAIR = 128
BLOCK = 128

epsilon = 1e-05
rope_base = 10000.0
negative = -1e30
f32 = jnp.float32
bf16 = jnp.bfloat16
LIMIT = 56 * 1024 * 1024

NN = (((1,), (0,)), ((), ()))
NT = (((1,), (1,)), ((), ()))
TN = (((0,), (0,)), ((), ()))


def mm(a, b, dims=NN):
    return lax.dot_general(a, b, dims, preferred_element_type=f32)


def unit_rows(x):
    center = x - jnp.mean(x, axis=-1, keepdims=True)
    inverse = lax.rsqrt(jnp.mean(center * center, axis=-1, keepdims=True) + epsilon)
    return center * inverse, inverse


def turn(x, cos, low, high):
    return x * cos + pltpu.roll(x, PAIR - 32, 1) * low + pltpu.roll(x, 32, 1) * high


def qkv_kernel(tok_ref, gain_ref, w_ref, cos_ref, low_ref, high_ref, q_ref, kv_ref):
    unit, _ = unit_rows(tok_ref[...].astype(f32))
    normed = (unit * gain_ref[...]).astype(bf16)
    cos, low, high = cos_ref[...], low_ref[...], high_ref[...]
    width = q_ref.shape[1]
    step = 2 * PAIR
    for j in range(3 * width // step):
        part = mm(normed, w_ref[:, j * step : (j + 1) * step])
        for h in range(2):
            at = j * step + h * PAIR
            piece = part[:, h * PAIR : (h + 1) * PAIR]
            if at < width:
                q_ref[:, at : at + PAIR] = (
                    turn(piece, cos, low, high) * (1.0 / math.sqrt(HEAD_DIM))
                ).astype(bf16)
            elif at < 2 * width:
                kv_ref[:, at - width : at - width + PAIR] = turn(piece, cos, low, high).astype(bf16)
            else:
                kv_ref[:, at - width : at - width + PAIR] = piece.astype(bf16)


def head_masks():
    lane = lax.broadcasted_iota(jnp.int32, (1, PAIR), 1)
    first = (lane < HEAD_DIM).astype(f32)
    return first.astype(bf16), (1.0 - first).astype(bf16), lane < HEAD_DIM


def fill(dst, left, mid, right):
    n = mid.shape[1]
    dst[0:WIN] = left[0]
    dst[WIN : WIN + n] = mid[0]
    dst[WIN + n : 2 * WIN + n] = right[0]


def attend_kernel(q_ref, k_ref, v_ref, lk_ref, lv_ref, rk_ref, rv_ref, bias_ref, att_ref, p_ref, ke, ve):
    fill(ke, lk_ref, k_ref, rk_ref)
    fill(ve, lv_ref, v_ref, rv_ref)
    first, second, is_first = head_masks()
    for i in range(q_ref.shape[1] // BLOCK):
        rows = slice(i * BLOCK, (i + 1) * BLOCK)
        span = slice(i * BLOCK, (i + 1) * BLOCK + 2 * WIN)
        query, key, value = q_ref[0, rows], ke[span], ve[span]
        outs = []
        for h, mask in enumerate((first, second)):
            scores = mm(query * mask, key, NT) + bias_ref[i]
            raised = jnp.exp(scores - jnp.max(scores, axis=-1, keepdims=True))
            total = jnp.sum(raised, axis=-1, keepdims=True)
            probs = (raised * (1.0 / total)).astype(bf16)
            p_ref[0, h, rows] = probs
            outs.append(mm(probs, value))
        att_ref[0, rows] = jnp.where(is_first, outs[0], outs[1]).astype(bf16)


def attend_back_kernel(
    q_ref, k_ref, v_ref, lk_ref, lv_ref, rk_ref, rv_ref, p_ref, ag_ref, cos_ref, low_ref, high_ref,
    dq_ref, dk_ref, dv_ref, dl_ref, dr_ref, ke, ve, ka, va,
):
    fill(ke, lk_ref, k_ref, rk_ref)
    fill(ve, lv_ref, v_ref, rv_ref)
    ka[...] = jnp.zeros_like(ka)
    va[...] = jnp.zeros_like(va)
    first, second, is_first = head_masks()
    count = q_ref.shape[1]
    scale = 1.0 / math.sqrt(HEAD_DIM)
    for i in range(count // BLOCK):
        rows = slice(i * BLOCK, (i + 1) * BLOCK)
        span = slice(i * BLOCK, (i + 1) * BLOCK + 2 * WIN)
        query, key, value, upstream = q_ref[0, rows], ke[span], ve[span], ag_ref[0, rows]
        dqs, dks, dvs = [], [], []
        for h, mask in enumerate((first, second)):
            low_probs = p_ref[0, h, rows]
            probs = low_probs.astype(f32)
            back = mm(upstream * mask, value, NT)
            weighted = probs * back
            delta = jnp.sum(weighted, axis=-1, keepdims=True)
            grad = (weighted - probs * delta).astype(bf16)
            dqs.append(mm(grad, key))
            dks.append(mm(grad, query, TN))
            dvs.append(mm(low_probs, upstream, TN))
        dq = jnp.where(is_first, dqs[0], dqs[1]) * scale
        at = slice(WIN + i * BLOCK, WIN + (i + 1) * BLOCK)
        dq_ref[0, rows] = turn(dq, cos_ref[at], -low_ref[at], -high_ref[at]).astype(bf16)
        ka[span] += jnp.where(is_first, dks[0], dks[1])
        va[span] += jnp.where(is_first, dvs[0], dvs[1])
    dk = turn(ka[...], cos_ref[...], -low_ref[...], -high_ref[...])
    dl_ref[0, 0] = dk[:WIN].astype(bf16)
    dk_ref[0] = dk[WIN : WIN + count].astype(bf16)
    dr_ref[0, 0] = dk[WIN + count :].astype(bf16)
    dl_ref[0, 1] = va[:WIN].astype(bf16)
    dv_ref[0] = va[WIN : WIN + count].astype(bf16)
    dr_ref[0, 1] = va[WIN + count :].astype(bf16)


def pack(dst, sources):
    shares, depth, width = dst.shape
    for f in range(shares):
        at = 0
        for src in sources:
            n = src.shape[0] // shares
            for j in range(src.shape[1] // width):
                dst[f, at : at + n] = src[f * n : (f + 1) * n, j * width : (j + 1) * width].astype(bf16)
                at += n
        if at < depth:
            dst[f, at:] = jnp.zeros((depth - at, width), bf16)


def unpack(share, shapes):
    width = share.shape[1]
    outs, at = [], 0
    for n, columns in shapes:
        parts = []
        for _ in range(columns // width):
            parts.append(share[at : at + n])
            at += n
        outs.append(jnp.concatenate(parts, axis=1) if len(parts) > 1 else parts[0])
    return outs


def padded_rows(n, seq_size):
    unit = 16 * seq_size
    return -(-n // unit) * unit


def mlp_kernel(
    tok_ref, att_ref, go_ref, gain_ref, wo_ref, win_ref, wout_ref,
    out_ref, mg_ref, ag_ref, pack_ref, dgain_ref,
    awo, awin, awout, wg_buf, hid_buf,
):
    step = pl.program_id(0)

    @pl.when(step == 0)
    def _():
        awo[...] = jnp.zeros_like(awo)
        awin[...] = jnp.zeros_like(awin)
        awout[...] = jnp.zeros_like(awout)
        dgain_ref[...] = jnp.zeros_like(dgain_ref)

    attended, go = att_ref[...], go_ref[...]
    middle = tok_ref[...].astype(f32) + mm(attended, wo_ref[...])
    gain = gain_ref[...]
    unit, inverse = unit_rows(middle)
    normed = (unit * gain).astype(bf16)
    chunk = 384
    for c in range(FF // chunk):
        cols = slice(c * chunk, (c + 1) * chunk)
        gate = slice(FF + c * chunk, FF + (c + 1) * chunk)
        a = mm(normed, win_ref[:, cols])
        b = mm(normed, win_ref[:, gate])
        hg = mm(go, wout_ref[cols, :], NT)
        cdf = 0.5 * (1.0 + lax.erf(a * (1.0 / math.sqrt(2.0))))
        gelu = a * cdf
        slope = cdf + a * (jnp.exp(-0.5 * a * a) * (1.0 / math.sqrt(2.0 * math.pi)))
        hid_buf[:, cols] = (gelu * b).astype(bf16)
        wg_buf[:, cols] = (hg * b * slope).astype(bf16)
        wg_buf[:, gate] = (hg * gelu).astype(bf16)
    hidden, wg = hid_buf[...], wg_buf[...]
    out_ref[...] = (middle + mm(hidden, wout_ref[...])).astype(bf16)
    back = mm(wg, win_ref[...], NT)
    dgain_ref[...] += jnp.sum(back * unit, axis=0, keepdims=True)
    e = back * gain
    part = e - jnp.mean(e, axis=-1, keepdims=True) - unit * jnp.mean(e * unit, axis=-1, keepdims=True)
    mg = go.astype(f32) + inverse * part
    mg_ref[...] = mg
    low = mg.astype(bf16)
    ag_ref[...] = mm(low, wo_ref[...], NT).astype(bf16)
    awout[...] += mm(hidden, go, TN)
    awin[...] += mm(normed, wg, TN)
    awo[...] += mm(attended, low, TN)

    @pl.when(step == pl.num_programs(0) - 1)
    def _():
        pack(pack_ref, (awin, awo, awout))


def qkv_back_kernel(
    tok_ref, mg_ref, dq_ref, dk_ref, dv_ref, fl_ref, fr_ref, gain_ref, w_ref,
    tg_ref, pack_ref, dgain_ref, acc, buf,
):
    step = pl.program_id(0)

    @pl.when(step == 0)
    def _():
        acc[...] = jnp.zeros_like(acc)
        dgain_ref[...] = jnp.zeros_like(dgain_ref)

    width = tok_ref.shape[2]
    count = tok_ref.shape[1]
    buf[:, :width] = dq_ref[0]
    for j, ref in enumerate((dk_ref, dv_ref)):
        cols = slice((j + 1) * width, (j + 2) * width)
        buf[:, cols] = ref[0]
        buf[:WIN, cols] = (ref[0, :WIN].astype(f32) + fl_ref[0, j].astype(f32)).astype(bf16)
        buf[count - WIN :, cols] = (
            ref[0, count - WIN :].astype(f32) + fr_ref[0, j].astype(f32)
        ).astype(bf16)
    gain = gain_ref[...]
    unit, inverse = unit_rows(tok_ref[0].astype(f32))
    normed = (unit * gain).astype(bf16)
    grads = buf[...]
    back = mm(grads, w_ref[...], NT)
    dgain_ref[...] += jnp.sum(back * unit, axis=0, keepdims=True)
    e = back * gain
    part = e - jnp.mean(e, axis=-1, keepdims=True) - unit * jnp.mean(e * unit, axis=-1, keepdims=True)
    tg_ref[0] = mg_ref[0] + inverse * part
    acc[...] += mm(normed, grads, TN)

    @pl.when(step == pl.num_programs(0) - 1)
    def _():
        pack(pack_ref, (acc,))


def gather_plan(shapes):
    plan = []
    for a, (n, columns) in enumerate(shapes):
        half = n // 2
        parts = 2 if half % 32 == 0 and n * columns > 300000 else 1
        plan += [(a, k * half // parts, half // parts) for k in range(parts)]
    return plan


def gather_kernel(*refs):
    ins, outs = refs[:4], refs[4:8]
    own_sem, xs, xr, ys, yr, cs, cr = refs[8:]
    plan = gather_plan([r.shape for r in ins])
    count = len(plan)
    seq, me = lax.axis_index("seq"), lax.axis_index("fsdp")
    across = lax.rem(me + 2, 4)
    core = me + 1 - 2 * lax.rem(me, 2)
    side = lax.rem(seq, 2)
    beside = {"seq": seq + 1 - 2 * side}
    barrier = pltpu.get_barrier_semaphore()
    for target in ({"fsdp": across}, {"fsdp": core}, beside):
        pl.semaphore_signal(barrier, inc=1, device_id=target, device_id_type=pl.DeviceIdType.MESH)
    pl.semaphore_wait(barrier, 3)

    def send(src, dst, ss, rs, target):
        copy = pltpu.make_async_remote_copy(
            src_ref=src, dst_ref=dst, send_sem=ss, recv_sem=rs,
            device_id=target, device_id_type=pl.DeviceIdType.MESH,
        )
        copy.start()
        return copy

    def place(a, owner, which, off, n):
        rows = ins[a].shape[0]
        at = owner * rows + which * (rows // 2) + off
        return outs[a].at[pl.ds(pl.multiple_of(at, 16), n)]

    def first_hop(k):
        a, off, n = plan[k]
        half = ins[a].shape[0] // 2
        src = ins[a].at[pl.ds(pl.multiple_of(side * half + off, 16), n)]
        return send(src, place(a, me, side, off, n), xs.at[k], xr.at[k], {"fsdp": across})

    hops = [first_hop(k) for k in range(count)]
    local, pairs = [], []
    for a in range(4):
        n = ins[a].shape[0]
        spot = outs[a].at[pl.ds(pl.multiple_of(me * n, 16), n)]
        copy = pltpu.make_async_copy(ins[a], spot, own_sem.at[a])
        copy.start()
        local.append(copy)
        pairs.append(send(ins[a], spot, cs.at[a], cr.at[a], {"fsdp": core}))
    seconds = []

    def relay(k):
        a, off, n = plan[k]
        seconds[k].wait_recv()
        spot = place(a, across, 1 - side, off, n)
        i = 4 + count + k
        pairs.append(send(spot, spot, cs.at[i], cr.at[i], {"fsdp": core}))

    for k in range(count):
        a, off, n = plan[k]
        hops[k].wait_recv()
        spot = place(a, across, side, off, n)
        seconds.append(send(spot, spot, ys.at[k], yr.at[k], beside))
        pairs.append(send(spot, spot, cs.at[4 + k], cr.at[4 + k], {"fsdp": core}))
        if k:
            relay(k - 1)
    relay(count - 1)
    for copy in local:
        copy.wait()
    for copy in hops + seconds:
        copy.wait_send()
    for copy in pairs:
        copy.wait_send()
        copy.wait_recv()


def gather_weights(*weights):
    count = len(gather_plan([w.shape for w in weights]))
    sems = lambda n: pltpu.SemaphoreType.DMA((n,))
    return pl.pallas_call(
        gather_kernel,
        in_specs=[pl.BlockSpec(memory_space=pl.ANY)] * 4,
        out_specs=[pl.BlockSpec(memory_space=pl.ANY)] * 4,
        out_shape=[sds((4 * w.shape[0], w.shape[1]), w.dtype) for w in weights],
        scratch_shapes=[sems(4)] + [sems(count)] * 4 + [sems(4 + 2 * count)] * 2,
        compiler_params=pltpu.CompilerParams(collective_id=0, has_side_effects=True),
        cost_estimate=pl.CostEstimate(flops=0, bytes_accessed=2**26, transcendentals=0),
        name="gather_weights",
    )(*weights)


def sds(shape, dtype):
    return jax.ShapeDtypeStruct(shape, dtype)


def whole(shape):
    return pl.BlockSpec(shape, lambda *_: (0,) * len(shape), pipeline_mode=pl.Buffered(1))


def tables(start, count):
    half = HEAD_DIM // 2
    freqs = rope_base ** (-(jnp.arange(half, dtype=f32) * 2.0 / HEAD_DIM))
    positions = (start + jnp.arange(count, dtype=jnp.int32)).astype(f32)
    angles = positions[:, None] * freqs[None, :]
    cos, sin = jnp.cos(angles), jnp.sin(angles)
    none = jnp.zeros_like(sin)
    return (
        jnp.concatenate([cos] * 4, axis=-1),
        jnp.concatenate([-sin, none] * 2, axis=-1),
        jnp.concatenate([none, sin] * 2, axis=-1),
    )


def shards(tokens, norm_gain_attn, qkv_weight, attn_out_weight, norm_gain_mlp, mlp_in_weight, mlp_out_weight, grad_out):
    seqs, piece, width = tokens.shape
    rows = seqs * piece
    span = piece + 2 * WIN
    pairs = width // PAIR
    seq_size = lax.axis_size("seq")
    shares = lax.axis_size("fsdp")
    mlp_shapes = (mlp_in_weight.shape, attn_out_weight.shape, mlp_out_weight.shape)
    mlp_rows = padded_rows(sum(n * m // width for n, m in mlp_shapes), seq_size)
    qkv_rows = padded_rows(3 * qkv_weight.shape[0] + 16, seq_size)
    forward = [(i, i + 1) for i in range(seq_size - 1)]
    backward = [(j, i) for i, j in forward]
    gains = lax.all_gather(jnp.stack([norm_gain_attn, norm_gain_mlp]), "fsdp", axis=1, tiled=True)
    w_qkv, w_attn, w_in, w_out = gather_weights(qkv_weight, attn_out_weight, mlp_in_weight, mlp_out_weight)
    gain_attn = gains[0:1].astype(f32)
    gain_mlp = gains[1:2].astype(f32)
    start = lax.axis_index("seq") * piece
    cos, low, high = tables(start - WIN, span)
    q_at = start + jnp.arange(piece, dtype=jnp.int32).reshape(-1, BLOCK)[:, :, None]
    k_at = (
        start - WIN
        + jnp.arange(piece // BLOCK, dtype=jnp.int32)[:, None, None] * BLOCK
        + jnp.arange(BLOCK + 2 * WIN, dtype=jnp.int32)[None, None, :]
    )
    inside = (jnp.abs(q_at - k_at) <= WIN) & (k_at >= 0) & (k_at < piece * seq_size)
    bias = jnp.where(inside, 0.0, negative).astype(f32)

    tile = 256
    per = piece // tile
    flat = lambda x: x.reshape(rows, x.shape[-1])
    row_spec = lambda w: pl.BlockSpec((tile, w), lambda i: (i, 0))
    table_spec = pl.BlockSpec((tile, PAIR), lambda i: (lax.rem(i, per), 0))
    params = lambda n: pltpu.CompilerParams(dimension_semantics=("arbitrary",) * n, vmem_limit_bytes=LIMIT)
    tok = flat(tokens)
    mid = slice(WIN, WIN + piece)
    q, kv = pl.pallas_call(
        qkv_kernel,
        grid=(rows // tile,),
        in_specs=[row_spec(width), whole((1, width)), whole(w_qkv.shape), table_spec, table_spec, table_spec],
        out_specs=[row_spec(width), row_spec(2 * width)],
        out_shape=[sds((rows, width), bf16), sds((rows, 2 * width), bf16)],
        compiler_params=params(1),
        cost_estimate=pl.CostEstimate(flops=6 * rows * width * width, bytes_accessed=12 * rows * width, transcendentals=0),
        name="qkv_forward",
    )(tok, gain_attn, w_qkv, cos[mid], low[mid], high[mid])
    q = q.reshape(seqs, piece, width)
    kv = kv.reshape(seqs, piece, 2 * width)
    left = lax.ppermute(kv[:, piece - WIN :], "seq", forward)
    right = lax.ppermute(kv[:, :WIN], "seq", backward)

    def lanes(n, off=0):
        return pl.BlockSpec((1, n, PAIR), lambda s, p: (s, 0, p + off))

    kv_specs = [
        lanes(piece), lanes(piece, pairs), lanes(WIN), lanes(WIN, pairs), lanes(WIN), lanes(WIN, pairs),
    ]
    kv_args = (kv, kv, left, left, right, right)
    p_spec = pl.BlockSpec((1, 2, piece, BLOCK + 2 * WIN), lambda s, p: (s, p, 0, 0))
    p_shape = (seqs, HEADS, piece, BLOCK + 2 * WIN)
    ext = pltpu.VMEM((span, PAIR), bf16)
    unit_flops = 2 * seqs * HEADS * piece * (BLOCK + 2 * WIN) * HEAD_DIM
    p_bytes = 2 * math.prod(p_shape)
    attended, probs = pl.pallas_call(
        attend_kernel,
        grid=(seqs, pairs),
        in_specs=[lanes(piece)] + kv_specs + [whole(bias.shape)],
        out_specs=[lanes(piece), p_spec],
        out_shape=[sds((seqs, piece, width), bf16), sds(p_shape, bf16)],
        scratch_shapes=[ext, ext],
        compiler_params=params(2),
        cost_estimate=pl.CostEstimate(flops=8 * unit_flops, bytes_accessed=p_bytes + 8 * rows * width, transcendentals=p_bytes // 2),
        name="attend_forward",
    )(q, *kv_args, bias)

    out, mg, ag, d_mlp, d_gain_mlp = pl.pallas_call(
        mlp_kernel,
        grid=(rows // tile,),
        in_specs=[row_spec(width)] * 3 + [whole((1, width)), whole(w_attn.shape), whole(w_in.shape), whole(w_out.shape)],
        out_specs=[row_spec(width)] * 3
        + [whole((shares, mlp_rows, width)), whole((1, width))],
        out_shape=[
            sds((rows, width), bf16), sds((rows, width), f32), sds((rows, width), bf16),
            sds((shares, mlp_rows, width), bf16), sds((1, width), f32),
        ],
        scratch_shapes=[
            pltpu.VMEM(w_attn.shape, f32), pltpu.VMEM(w_in.shape, f32), pltpu.VMEM(w_out.shape, f32),
            pltpu.VMEM((tile, 2 * FF), bf16), pltpu.VMEM((tile, FF), bf16),
        ],
        compiler_params=params(1),
        cost_estimate=pl.CostEstimate(flops=6 * rows * width * (width + 3 * FF), bytes_accessed=40 * 2**20, transcendentals=0),
        name="mlp_both_ways",
    )(tok, flat(attended), flat(grad_out), gain_mlp, w_attn, w_in, w_out)

    def reduce(x):
        mine = lax.psum_scatter(x, "fsdp", scatter_dimension=0, tiled=True)[0]
        part = lax.psum_scatter(mine, "seq", scatter_dimension=0, tiled=True)
        return lax.all_gather(part, "seq", axis=0, tiled=True)

    mlp_sum = reduce(d_mlp)

    table_full = pl.BlockSpec((span, PAIR), lambda s, p: (0, 0))
    edge = pl.BlockSpec((1, 2, WIN, PAIR), lambda s, p: (s, 0, 0, p))
    edge_shape = sds((seqs, 2, WIN, width), bf16)
    own = sds((seqs, piece, width), bf16)
    total = pltpu.VMEM((span, PAIR), f32)
    dq, dk, dv, dl, dr = pl.pallas_call(
        attend_back_kernel,
        grid=(seqs, pairs),
        in_specs=[lanes(piece)] + kv_specs + [p_spec, lanes(piece), table_full, table_full, table_full],
        out_specs=[lanes(piece)] * 3 + [edge, edge],
        out_shape=[own] * 3 + [edge_shape] * 2,
        scratch_shapes=[ext, ext, total, total],
        compiler_params=params(2),
        cost_estimate=pl.CostEstimate(flops=16 * unit_flops, bytes_accessed=p_bytes + 16 * rows * width, transcendentals=0),
        name="attend_backward",
    )(q, *kv_args, probs, ag.reshape(seqs, piece, width), cos, low, high)
    from_left = lax.ppermute(dr, "seq", forward)
    from_right = lax.ppermute(dl, "seq", backward)

    seq_spec = pl.BlockSpec((1, piece, width), lambda s: (s, 0, 0))
    edge_in = pl.BlockSpec((1, 2, WIN, width), lambda s: (s, 0, 0, 0))
    tokens_grad, d_wqkv, d_gain_attn = pl.pallas_call(
        qkv_back_kernel,
        grid=(seqs,),
        in_specs=[seq_spec] * 5 + [edge_in] * 2 + [whole((1, width)), whole(w_qkv.shape)],
        out_specs=[seq_spec, whole((shares, qkv_rows, width)), whole((1, width))],
        out_shape=[sds((seqs, piece, width), f32), sds((shares, qkv_rows, width), bf16), sds((1, width), f32)],
        scratch_shapes=[pltpu.VMEM(w_qkv.shape, f32), pltpu.VMEM((piece, 3 * width), bf16)],
        compiler_params=params(1),
        cost_estimate=pl.CostEstimate(flops=12 * rows * width * width, bytes_accessed=20 * rows * width, transcendentals=0),
        name="qkv_backward",
    )(tokens, mg.reshape(seqs, piece, width), dq, dk, dv, from_left, from_right, gain_attn, w_qkv)

    gains_at = 3 * qkv_weight.shape[0]
    both = jnp.concatenate([d_gain_attn, d_gain_mlp]).astype(bf16)
    both = both.reshape(2, shares, width // shares).swapaxes(0, 1)
    both = jnp.pad(both, ((0, 0), (0, 0), (0, width - width // shares)))
    d_wqkv = lax.dynamic_update_slice(d_wqkv, both, (0, gains_at, 0))
    qkv_sum = reduce(d_wqkv)
    s_wqkv = unpack(qkv_sum, (qkv_weight.shape,))[0]
    s_gains = qkv_sum[gains_at : gains_at + 2, : width // shares].astype(f32)
    s_win, s_wo, s_wout = unpack(mlp_sum, mlp_shapes)
    return (
        out.reshape(seqs, piece, width),
        tokens_grad,
        s_gains[0],
        s_wqkv.astype(f32),
        s_wo.astype(f32),
        s_gains[1],
        s_win.astype(f32),
        s_wout.astype(f32),
    )


def solution(mesh):
    return jax.shard_map(
        shards,
        mesh=mesh,
        in_specs=(
            P("fsdp", "seq", None),
            P("fsdp"),
            P("fsdp", None),
            P("fsdp", None),
            P("fsdp"),
            P("fsdp", None),
            P("fsdp", None),
            P("fsdp", "seq", None),
        ),
        out_specs=(
            P("fsdp", "seq", None),
            P("fsdp", "seq", None),
            P("fsdp"),
            P("fsdp", None),
            P("fsdp", None),
            P("fsdp"),
            P("fsdp", None),
            P("fsdp", None),
        ),
        check_vma=False,
    )
```

```python
import functools
import math

import jax
import jax.numpy as jnp
from jax import lax
from jax.experimental import pallas as pl
from jax.experimental.pallas import tpu as pltpu
from jax.sharding import PartitionSpec as P

HEADS = 12
HEAD_DIM = 64
FF = 1152
WIN = 64
PAIR = 128
BLOCK = 128

epsilon = 1e-05
rope_base = 10000.0
negative = -1e30
f32 = jnp.float32
bf16 = jnp.bfloat16
LIMIT = 56 * 1024 * 1024

NN = (((1,), (0,)), ((), ()))
NT = (((1,), (1,)), ((), ()))
TN = (((0,), (0,)), ((), ()))


def mm(a, b, dims=NN):
    return lax.dot_general(a, b, dims, preferred_element_type=f32)


def unit_rows(x):
    center = x - jnp.mean(x, axis=-1, keepdims=True)
    inverse = lax.rsqrt(jnp.mean(center * center, axis=-1, keepdims=True) + epsilon)
    return center * inverse, inverse


def turn(x, cos, low, high):
    return x * cos + pltpu.roll(x, PAIR - 32, 1) * low + pltpu.roll(x, 32, 1) * high


def qkv_kernel(tok_ref, gain_ref, w_ref, cos_ref, low_ref, high_ref, q_ref, kv_ref):
    unit, _ = unit_rows(tok_ref[...].astype(f32))
    normed = (unit * gain_ref[...]).astype(bf16)
    cos, low, high = cos_ref[...], low_ref[...], high_ref[...]
    width = q_ref.shape[1]
    step = 2 * PAIR
    for j in range(3 * width // step):
        part = mm(normed, w_ref[:, j * step : (j + 1) * step])
        for h in range(2):
            at = j * step + h * PAIR
            piece = part[:, h * PAIR : (h + 1) * PAIR]
            if at < width:
                q_ref[:, at : at + PAIR] = (
                    turn(piece, cos, low, high) * (1.0 / math.sqrt(HEAD_DIM))
                ).astype(bf16)
            elif at < 2 * width:
                kv_ref[:, at - width : at - width + PAIR] = turn(piece, cos, low, high).astype(bf16)
            else:
                kv_ref[:, at - width : at - width + PAIR] = piece.astype(bf16)


def by_head(x):
    first = (lax.broadcasted_iota(jnp.int32, (1, PAIR), 1) < HEAD_DIM).astype(f32)
    return jnp.concatenate([x * first.astype(bf16), x * (1.0 - first).astype(bf16)], axis=0)


def own_heads(x):
    both = jnp.concatenate([x[:HEAD_DIM, :BLOCK], x[HEAD_DIM:, BLOCK:]], axis=0)
    return both.T


def fill(dst, left, mid, right):
    n = mid.shape[1]
    dst[0:WIN] = left[0]
    dst[WIN : WIN + n] = mid[0]
    dst[WIN + n : 2 * WIN + n] = right[0]


def attend_kernel(q_ref, k_ref, v_ref, lk_ref, lv_ref, rk_ref, rv_ref, bias_ref, att_ref, p_ref, ke, ve):
    fill(ke, lk_ref, k_ref, rk_ref)
    fill(ve, lv_ref, v_ref, rv_ref)
    vt = ve[...].T
    for i in range(q_ref.shape[1] // BLOCK):
        rows = slice(i * BLOCK, (i + 1) * BLOCK)
        span = slice(i * BLOCK, (i + 1) * BLOCK + 2 * WIN)
        scores = mm(ke[span], by_head(q_ref[0, rows]), NT)
        scores = scores + jnp.concatenate([bias_ref[i]] * 2, axis=1)
        raised = jnp.exp(scores - jnp.max(scores, axis=0, keepdims=True))
        total = jnp.sum(raised, axis=0, keepdims=True)
        probs = (raised * (1.0 / total)).astype(bf16)
        p_ref[0, 0, i] = probs
        att_ref[0, rows] = own_heads(mm(vt[:, span], probs)).astype(bf16)


def attend_back_kernel(
    q_ref, k_ref, v_ref, lk_ref, lv_ref, rk_ref, rv_ref, p_ref, ag_ref, cos_ref, low_ref, high_ref,
    dq_ref, dk_ref, dv_ref, dl_ref, dr_ref, ke, ve, ka, va,
):
    fill(ke, lk_ref, k_ref, rk_ref)
    fill(ve, lv_ref, v_ref, rv_ref)
    ka[...] = jnp.zeros_like(ka)
    va[...] = jnp.zeros_like(va)
    count = q_ref.shape[1]
    scale = 1.0 / math.sqrt(HEAD_DIM)
    kt = ke[...].T
    for i in range(count // BLOCK):
        rows = slice(i * BLOCK, (i + 1) * BLOCK)
        span = slice(i * BLOCK, (i + 1) * BLOCK + 2 * WIN)
        upstream = by_head(ag_ref[0, rows])
        low_probs = p_ref[0, 0, i]
        probs = low_probs.astype(f32)
        back = mm(ve[span], upstream, NT)
        delta = jnp.sum(probs * back, axis=0, keepdims=True)
        grad = (probs * (back - delta)).astype(bf16)
        dq = own_heads(mm(kt[:, span], grad)) * scale
        at = slice(WIN + i * BLOCK, WIN + (i + 1) * BLOCK)
        dq_ref[0, rows] = turn(dq, cos_ref[at], -low_ref[at], -high_ref[at]).astype(bf16)
        ka[span] += mm(grad, by_head(q_ref[0, rows]))
        va[span] += mm(low_probs, upstream)
    dk = turn(ka[...], cos_ref[...], -low_ref[...], -high_ref[...])
    dl_ref[0, 0] = dk[:WIN].astype(bf16)
    dk_ref[0] = dk[WIN : WIN + count].astype(bf16)
    dr_ref[0, 0] = dk[WIN + count :].astype(bf16)
    dl_ref[0, 1] = va[:WIN].astype(bf16)
    dv_ref[0] = va[WIN : WIN + count].astype(bf16)
    dr_ref[0, 1] = va[WIN + count :].astype(bf16)


def unpack(share, shapes):
    width = share.shape[1]
    outs, at = [], 0
    for n, columns in shapes:
        parts = []
        for _ in range(columns // width):
            parts.append(share[at : at + n])
            at += n
        outs.append(jnp.concatenate(parts, axis=1) if len(parts) > 1 else parts[0])
    return outs


def padded_rows(n, seq_size):
    unit = 16 * seq_size
    return -(-n // unit) * unit


def mlp_kernel(
    steps,
    tok_ref, att_ref, go_ref, gain_ref, wo_ref, win_ref, wout_ref,
    out_ref, mg_ref, ag_ref, pack_ref, dgain_ref,
    awo, awin, awout, wg_buf, hid_buf,
):
    step = pl.program_id(0)

    @pl.when(step == 0)
    def _():
        dgain_ref[...] = jnp.zeros_like(dgain_ref)

    attended, go = att_ref[...], go_ref[...]
    middle = tok_ref[...].astype(f32) + mm(attended, wo_ref[...])
    gain = gain_ref[...]
    unit, inverse = unit_rows(middle)
    normed = (unit * gain).astype(bf16)
    chunk = 384
    for c in range(FF // chunk):
        cols = slice(c * chunk, (c + 1) * chunk)
        gate = slice(FF + c * chunk, FF + (c + 1) * chunk)
        a = mm(normed, win_ref[:, cols])
        b = mm(normed, win_ref[:, gate])
        hg = mm(go, wout_ref[cols, :], NT)
        cdf = 0.5 * (1.0 + lax.erf(a * (1.0 / math.sqrt(2.0))))
        gelu = a * cdf
        slope = cdf + a * (jnp.exp(-0.5 * a * a) * (1.0 / math.sqrt(2.0 * math.pi)))
        hid_buf[:, cols] = (gelu * b).astype(bf16)
        wg_buf[:, cols] = (hg * b * slope).astype(bf16)
        wg_buf[:, gate] = (hg * gelu).astype(bf16)
    hidden, wg = hid_buf[...], wg_buf[...]
    out_ref[...] = (middle + mm(hidden, wout_ref[...])).astype(bf16)
    back = mm(wg, win_ref[...], NT)
    dgain_ref[...] += jnp.sum(back * unit, axis=0, keepdims=True)
    e = back * gain
    part = e - jnp.mean(e, axis=-1, keepdims=True) - unit * jnp.mean(e * unit, axis=-1, keepdims=True)
    mg = go.astype(f32) + inverse * part
    mg_ref[...] = mg
    low = mg.astype(bf16)
    ag_ref[...] = mm(low, wo_ref[...], NT).astype(bf16)
    products = ((awin, normed, wg), (awo, attended, low), (awout, hidden, go))
    last = steps - 1

    @pl.when(step == 0)
    def _():
        for acc, lhs, rhs in products:
            acc[...] = mm(lhs, rhs, TN)

    if steps > 2:

        @pl.when((step > 0) & (step < last))
        def _():
            for acc, lhs, rhs in products:
                acc[...] += mm(lhs, rhs, TN)

    @pl.when(step == last)
    def _():
        shares, depth, width = pack_ref.shape
        at = 0
        for acc, lhs, rhs in products:
            n = acc.shape[0] // shares
            for j in range(acc.shape[1] // width):
                cols = slice(j * width, (j + 1) * width)
                for f in range(shares):
                    mine = slice(f * n, (f + 1) * n)
                    piece = mm(lhs[:, mine], rhs[:, cols], TN) + acc[mine, cols]
                    pack_ref[f, at : at + n] = piece.astype(bf16)
                at += n
        if at < depth:
            for f in range(shares):
                pack_ref[f, at:] = jnp.zeros((depth - at, width), bf16)


def qkv_back_kernel(
    prior, kept, last, tok_ref, mg_ref, dq_ref, dk_ref, dv_ref, fl_ref, fr_ref, gain_ref, w_ref, *refs
):
    tg_ref, dw_ref, dgain_ref, buf = refs[prior + kept :]
    width = tok_ref.shape[2]
    count = tok_ref.shape[1]
    buf[:, :width] = dq_ref[0]
    for j, ref in enumerate((dk_ref, dv_ref)):
        cols = slice((j + 1) * width, (j + 2) * width)
        buf[:, cols] = ref[0]
        buf[:WIN, cols] = (ref[0, :WIN].astype(f32) + fl_ref[0, j].astype(f32)).astype(bf16)
        buf[count - WIN :, cols] = (
            ref[0, count - WIN :].astype(f32) + fr_ref[0, j].astype(f32)
        ).astype(bf16)
    gain = gain_ref[...]
    unit, inverse = unit_rows(tok_ref[0].astype(f32))
    normed = (unit * gain).astype(bf16)
    grads = buf[...]
    back = mm(grads, w_ref[...], NT)
    gain_grad = jnp.sum(back * unit, axis=0, keepdims=True)
    dgain_ref[...] = gain_grad + refs[1][...] if prior else gain_grad
    e = back * gain
    part = e - jnp.mean(e, axis=-1, keepdims=True) - unit * jnp.mean(e * unit, axis=-1, keepdims=True)
    tg_ref[0] = mg_ref[0] + inverse * part
    for j in range(3):
        cols = slice(j * width, (j + 1) * width)
        piece = mm(normed, grads[:, cols], TN)
        if prior:
            piece = piece + refs[0][:, cols].astype(f32)
        if not last:
            dw_ref[:, cols] = piece.astype(bf16)
            continue
        shares = dw_ref.shape[0]
        n = piece.shape[0] // shares
        for f in range(shares):
            dw_ref[f, j * n : (j + 1) * n] = piece[f * n : (f + 1) * n].astype(bf16)
    if last:
        at = 3 * w_ref.shape[0] // dw_ref.shape[0]
        dw_ref[:, at:] = jnp.zeros((dw_ref.shape[0], dw_ref.shape[1] - at, width), bf16)


def reduce_kernel(pack_ref, out_ref, mine, got, total, far, ls, cs, cr, xs, xr):
    me = lax.axis_index("fsdp")
    across = lax.rem(me + 2, 4)
    core = me + 1 - 2 * lax.rem(me, 2)
    barrier = pltpu.get_barrier_semaphore()
    for target in (across, core):
        pl.semaphore_signal(
            barrier, inc=1, device_id={"fsdp": target}, device_id_type=pl.DeviceIdType.MESH
        )
    pl.semaphore_wait(barrier, 2)
    parts = xs.shape[0]
    n = out_ref.shape[0] // parts
    rows = [pl.ds(k * n, n) for k in range(parts)]

    def send(src, dst, ss, rs, target):
        copy = pltpu.make_async_remote_copy(
            src_ref=src, dst_ref=dst, send_sem=ss, recv_sem=rs,
            device_id={"fsdp": target}, device_id_type=pl.DeviceIdType.MESH,
        )
        copy.start()
        return copy

    pairs, locals_ = {}, {}
    for slot, theirs, ours in ((0, lax.rem(core + 2, 4), across), (1, core, me)):
        for k in range(parts):
            i = slot * parts + k
            pairs[slot, k] = send(pack_ref.at[theirs, rows[k]], got.at[slot, rows[k]], cs.at[i], cr.at[i], core)
            copy = pltpu.make_async_copy(pack_ref.at[ours, rows[k]], mine.at[slot, rows[k]], ls.at[i])
            copy.start()
            locals_[slot, k] = copy
    hops = []
    for k in range(parts):
        locals_[0, k].wait()
        pairs[0, k].wait_recv()
        total[rows[k]] = (mine[0, rows[k]].astype(f32) + got[0, rows[k]].astype(f32)).astype(bf16)
        hops.append(send(total.at[rows[k]], far.at[rows[k]], xs.at[k], xr.at[k], across))
    for k in range(parts):
        locals_[1, k].wait()
        pairs[1, k].wait_recv()
        hops[k].wait_recv()
        out_ref[rows[k]] = (
            mine[1, rows[k]].astype(f32) + got[1, rows[k]].astype(f32) + far[rows[k]].astype(f32)
        ).astype(bf16)
    for copy in list(pairs.values()) + hops:
        copy.wait_send()


def reduce_fsdp(x, parts):
    shares, n, width = x.shape
    sems = lambda m: pltpu.SemaphoreType.DMA((m,))
    vmem = lambda *shape: pltpu.VMEM(shape, bf16)
    return pl.pallas_call(
        reduce_kernel,
        in_specs=[pl.BlockSpec(memory_space=pl.ANY)],
        out_specs=pl.BlockSpec(memory_space=pltpu.VMEM),
        out_shape=sds((n, width), bf16),
        scratch_shapes=[vmem(2, n, width), vmem(2, n, width), vmem(n, width), vmem(n, width)]
        + [sems(2 * parts)] * 3 + [sems(parts)] * 2,
        compiler_params=pltpu.CompilerParams(collective_id=1, has_side_effects=True, vmem_limit_bytes=LIMIT),
        cost_estimate=pl.CostEstimate(flops=0, bytes_accessed=2**26, transcendentals=0),
        name="reduce_fsdp",
    )(x)


def sds(shape, dtype):
    return jax.ShapeDtypeStruct(shape, dtype)


def whole(shape):
    return pl.BlockSpec(shape, lambda *_: (0,) * len(shape), pipeline_mode=pl.Buffered(1))


def tables(start, count):
    half = HEAD_DIM // 2
    freqs = rope_base ** (-(jnp.arange(half, dtype=f32) * 2.0 / HEAD_DIM))
    positions = (start + jnp.arange(count, dtype=jnp.int32)).astype(f32)
    angles = positions[:, None] * freqs[None, :]
    cos, sin = jnp.cos(angles), jnp.sin(angles)
    none = jnp.zeros_like(sin)
    return (
        jnp.concatenate([cos] * 4, axis=-1),
        jnp.concatenate([-sin, none] * 2, axis=-1),
        jnp.concatenate([none, sin] * 2, axis=-1),
    )


def shards(tokens, norm_gain_attn, qkv_weight, attn_out_weight, norm_gain_mlp, mlp_in_weight, mlp_out_weight, grad_out):
    seqs, piece, width = tokens.shape
    rows = seqs * piece
    span = piece + 2 * WIN
    pairs = width // PAIR
    seq_size = lax.axis_size("seq")
    shares = lax.axis_size("fsdp")
    mlp_shapes = (mlp_in_weight.shape, attn_out_weight.shape, mlp_out_weight.shape)
    mlp_rows = sum(n * m // width for n, m in mlp_shapes)
    qkv_rows = padded_rows(3 * qkv_weight.shape[0] + 16, seq_size)
    forward = [(i, i + 1) for i in range(seq_size - 1)]
    backward = [(j, i) for i, j in forward]
    gains = lax.all_gather(jnp.stack([norm_gain_attn, norm_gain_mlp]), "fsdp", axis=1, tiled=True)
    gather = lambda x: lax.all_gather(x, "fsdp", axis=0, tiled=True)
    w_qkv = gather(qkv_weight)
    w_attn = gather(attn_out_weight)
    w_in = gather(mlp_in_weight)
    w_out = gather(mlp_out_weight)
    gain_attn = gains[0:1].astype(f32)
    gain_mlp = gains[1:2].astype(f32)
    start = lax.axis_index("seq") * piece
    cos, low, high = tables(start - WIN, span)
    q_at = start + jnp.arange(piece, dtype=jnp.int32).reshape(-1, BLOCK)[:, None, :]
    k_at = (
        start - WIN
        + jnp.arange(piece // BLOCK, dtype=jnp.int32)[:, None, None] * BLOCK
        + jnp.arange(BLOCK + 2 * WIN, dtype=jnp.int32)[None, :, None]
    )
    inside = (jnp.abs(q_at - k_at) <= WIN) & (k_at >= 0) & (k_at < piece * seq_size)
    bias = jnp.where(inside, 0.0, negative).astype(f32)

    tile = 256
    per = piece // tile
    flat = lambda x: x.reshape(rows, x.shape[-1])
    row_spec = lambda w: pl.BlockSpec((tile, w), lambda i: (i, 0))
    table_spec = pl.BlockSpec((tile, PAIR), lambda i: (lax.rem(i, per), 0))
    params = lambda n: pltpu.CompilerParams(dimension_semantics=("arbitrary",) * n, vmem_limit_bytes=LIMIT)
    tok = flat(tokens)
    mid = slice(WIN, WIN + piece)
    def project(x, *rotary):
        count = x.shape[0]
        return pl.pallas_call(
            qkv_kernel,
            grid=(count // tile,),
            in_specs=[row_spec(width), whole((1, width)), whole(w_qkv.shape), table_spec, table_spec, table_spec],
            out_specs=[row_spec(width), row_spec(2 * width)],
            out_shape=[sds((count, width), bf16), sds((count, 2 * width), bf16)],
            compiler_params=params(1),
            cost_estimate=pl.CostEstimate(flops=6 * count * width * width, bytes_accessed=12 * count * width, transcendentals=0),
            name="qkv_forward",
        )(x, gain_attn, w_qkv, *rotary)

    borders = lambda x, n: jnp.concatenate([x[..., :WIN, :], x[..., n - WIN :, :]], axis=-2)
    _, kv_border = project(
        borders(tokens, piece).reshape(-1, width),
        *(jnp.tile(borders(t[mid], piece), (seqs, 1)) for t in (cos, low, high)),
    )
    kv_border = kv_border.reshape(seqs, 2 * WIN, 2 * width)
    left = lax.ppermute(kv_border[:, WIN:], "seq", forward)
    right = lax.ppermute(kv_border[:, :WIN], "seq", backward)
    q, kv = project(tok, cos[mid], low[mid], high[mid])
    q = q.reshape(seqs, piece, width)
    kv = kv.reshape(seqs, piece, 2 * width)

    def lanes(n, off=0):
        return pl.BlockSpec((1, n, PAIR), lambda s, p: (s, 0, p + off))

    kv_specs = [
        lanes(piece), lanes(piece, pairs), lanes(WIN), lanes(WIN, pairs), lanes(WIN), lanes(WIN, pairs),
    ]
    kv_args = (kv, kv, left, left, right, right)
    p_block = (1, 1, piece // BLOCK, BLOCK + 2 * WIN, 2 * BLOCK)
    p_spec = pl.BlockSpec(p_block, lambda s, p: (s, p, 0, 0, 0))
    p_shape = (seqs, pairs) + p_block[2:]
    ext = pltpu.VMEM((span, PAIR), bf16)
    unit_flops = 2 * seqs * HEADS * piece * (BLOCK + 2 * WIN) * HEAD_DIM
    p_bytes = 2 * math.prod(p_shape)
    attended, probs = pl.pallas_call(
        attend_kernel,
        grid=(seqs, pairs),
        in_specs=[lanes(piece)] + kv_specs + [whole(bias.shape)],
        out_specs=[lanes(piece), p_spec],
        out_shape=[sds((seqs, piece, width), bf16), sds(p_shape, bf16)],
        scratch_shapes=[ext, ext],
        compiler_params=params(2),
        cost_estimate=pl.CostEstimate(flops=8 * unit_flops, bytes_accessed=p_bytes + 8 * rows * width, transcendentals=p_bytes // 2),
        name="attend_forward",
    )(q, *kv_args, bias)

    wide = piece
    wide_spec = pl.BlockSpec((wide, width), lambda i: (i, 0))
    out, mg, ag, d_mlp, d_gain_mlp = pl.pallas_call(
        functools.partial(mlp_kernel, rows // wide),
        grid=(rows // wide,),
        in_specs=[wide_spec] * 3 + [whole((1, width)), whole(w_attn.shape), whole(w_in.shape), whole(w_out.shape)],
        out_specs=[wide_spec] * 3
        + [whole((shares, mlp_rows, width)), whole((1, width))],
        out_shape=[
            sds((rows, width), bf16), sds((rows, width), f32), sds((rows, width), bf16),
            sds((shares, mlp_rows, width), bf16), sds((1, width), f32),
        ],
        scratch_shapes=[
            pltpu.VMEM(w_attn.shape, f32), pltpu.VMEM(w_in.shape, f32), pltpu.VMEM(w_out.shape, f32),
            pltpu.VMEM((wide, 2 * FF), bf16), pltpu.VMEM((wide, FF), bf16),
        ],
        compiler_params=params(1),
        cost_estimate=pl.CostEstimate(flops=6 * rows * width * (width + 3 * FF), bytes_accessed=40 * 2**20, transcendentals=0),
        name="mlp_both_ways",
    )(tok, flat(attended), flat(grad_out), gain_mlp, w_attn, w_in, w_out)

    mlp_sum = lax.psum(lax.psum_scatter(d_mlp, "fsdp", scatter_dimension=0, tiled=True)[0], "seq")

    table_full = pl.BlockSpec((span, PAIR), lambda p: (0, 0))
    edge_shape = sds((1, 2, WIN, width), bf16)
    own = sds((1, piece, width), bf16)
    total = pltpu.VMEM((span, PAIR), f32)
    ag = ag.reshape(seqs, piece, width)
    mg = mg.reshape(seqs, piece, width)

    def attend_back(s):
        def at(n, off=0):
            return pl.BlockSpec((1, n, PAIR), lambda p: (s, 0, p + off))

        here = pl.BlockSpec((1, piece, PAIR), lambda p: (0, 0, p))
        edge = pl.BlockSpec((1, 2, WIN, PAIR), lambda p: (0, 0, 0, p))
        return pl.pallas_call(
            attend_back_kernel,
            grid=(pairs,),
            in_specs=[at(piece), at(piece), at(piece, pairs), at(WIN), at(WIN, pairs), at(WIN), at(WIN, pairs)]
            + [pl.BlockSpec(p_block, lambda p: (s, p, 0, 0, 0)), at(piece)]
            + [table_full] * 3,
            out_specs=[here] * 3 + [edge, edge],
            out_shape=[own] * 3 + [edge_shape] * 2,
            scratch_shapes=[ext, ext, total, total],
            compiler_params=params(1),
            cost_estimate=pl.CostEstimate(flops=8 * unit_flops, bytes_accessed=p_bytes // 2 + 8 * rows * width, transcendentals=0),
            name="attend_backward",
        )(q, *kv_args, probs, ag, cos, low, high)

    one = pl.BlockSpec((1, piece, width), lambda i: (0, 0, 0))
    edge_in = pl.BlockSpec((1, 2, WIN, width), lambda i: (0, 0, 0, 0))

    def qkv_back(s, grads, before, tokens_grad):
        this = pl.BlockSpec((1, piece, width), lambda i: (s, 0, 0))
        last = s == seqs - 1
        prior = [] if before is None else list(before)
        to = (shares, qkv_rows, width) if last else w_qkv.shape
        kept = [] if tokens_grad is None else [tokens_grad]
        args = [tokens, mg, *grads, gain_attn, w_qkv, *prior, *kept]
        return pl.pallas_call(
            functools.partial(qkv_back_kernel, len(prior), len(kept), last),
            grid=(1,),
            in_specs=[this] * 2 + [one] * 3 + [edge_in] * 2 + [whole((1, width)), whole(w_qkv.shape)]
            + [whole(p.shape) for p in prior] + [pl.BlockSpec(memory_space=pl.ANY)] * len(kept),
            out_specs=[this, whole(to), whole((1, width))],
            out_shape=[sds(tokens.shape, f32), sds(to, bf16), sds((1, width), f32)],
            scratch_shapes=[pltpu.VMEM((piece, 3 * width), bf16)],
            input_output_aliases={len(args) - 1: 0} if kept else {},
            compiler_params=params(1),
            cost_estimate=pl.CostEstimate(flops=12 * piece * width * width, bytes_accessed=20 * piece * width, transcendentals=0),
            name="qkv_backward",
        )(*args)

    grads = []
    for s in range(seqs):
        dq, dk, dv, dl, dr = attend_back(s)
        grads.append((dq, dk, dv, lax.ppermute(dr, "seq", forward), lax.ppermute(dl, "seq", backward)))
    before = tokens_grad = None
    for s in range(seqs):
        tokens_grad, *before = qkv_back(s, grads[s], before, tokens_grad)
    d_wqkv, d_gain_attn = before

    gains_at = 3 * qkv_weight.shape[0]
    both = jnp.concatenate([d_gain_attn, d_gain_mlp]).astype(bf16)
    both = both.reshape(2, shares, width // shares).swapaxes(0, 1)
    both = jnp.pad(both, ((0, 0), (0, 0), (0, width - width // shares)))
    d_wqkv = lax.dynamic_update_slice(d_wqkv, both, (0, gains_at, 0))
    qkv_share, mlp_sum = lax.optimization_barrier((reduce_fsdp(d_wqkv, 4), mlp_sum))
    qkv_sum = lax.psum(qkv_share, "seq")
    s_wqkv = unpack(qkv_sum, (qkv_weight.shape,))[0]
    s_gains = qkv_sum[gains_at : gains_at + 2, : width // shares].astype(f32)
    s_win, s_wo, s_wout = unpack(mlp_sum, mlp_shapes)
    return (
        out.reshape(seqs, piece, width),
        tokens_grad,
        s_gains[0],
        s_wqkv.astype(f32),
        s_wo.astype(f32),
        s_gains[1],
        s_win.astype(f32),
        s_wout.astype(f32),
    )


def solution(mesh):
    return jax.shard_map(
        shards,
        mesh=mesh,
        in_specs=(
            P("fsdp", "seq", None),
            P("fsdp"),
            P("fsdp", None),
            P("fsdp", None),
            P("fsdp"),
            P("fsdp", None),
            P("fsdp", None),
            P("fsdp", "seq", None),
        ),
        out_specs=(
            P("fsdp", "seq", None),
            P("fsdp", "seq", None),
            P("fsdp"),
            P("fsdp", None),
            P("fsdp", None),
            P("fsdp"),
            P("fsdp", None),
            P("fsdp", None),
        ),
        check_vma=False,
    )
```

```python
import functools
import math

import jax
import jax.numpy as jnp
from jax import lax
from jax.experimental import pallas as pl
from jax.experimental.pallas import tpu as pltpu
from jax.sharding import PartitionSpec as P

HEADS = 12
HEAD_DIM = 64
FF = 1152
WIN = 64
PAIR = 128
BLOCK = 128

epsilon = 1e-05
rope_base = 10000.0
negative = -1e30
f32 = jnp.float32
bf16 = jnp.bfloat16
LIMIT = 56 * 1024 * 1024

NN = (((1,), (0,)), ((), ()))
NT = (((1,), (1,)), ((), ()))
TN = (((0,), (0,)), ((), ()))


def mm(a, b, dims=NN):
    return lax.dot_general(a, b, dims, preferred_element_type=f32)


def unit_rows(x):
    center = x - jnp.mean(x, axis=-1, keepdims=True)
    inverse = lax.rsqrt(jnp.mean(center * center, axis=-1, keepdims=True) + epsilon)
    return center * inverse, inverse


def turn(x, cos, low, high):
    return x * cos + pltpu.roll(x, PAIR - 32, 1) * low + pltpu.roll(x, 32, 1) * high


def qkv_kernel(tok_ref, gain_ref, w_ref, cos_ref, low_ref, high_ref, q_ref, kv_ref):
    unit, _ = unit_rows(tok_ref[...].astype(f32))
    normed = (unit * gain_ref[...]).astype(bf16)
    cos, low, high = cos_ref[...], low_ref[...], high_ref[...]
    width = q_ref.shape[1]
    step = 2 * PAIR
    for j in range(3 * width // step):
        part = mm(normed, w_ref[:, j * step : (j + 1) * step])
        for h in range(2):
            at = j * step + h * PAIR
            piece = part[:, h * PAIR : (h + 1) * PAIR]
            if at < width:
                q_ref[:, at : at + PAIR] = (
                    turn(piece, cos, low, high) * (1.0 / math.sqrt(HEAD_DIM))
                ).astype(bf16)
            elif at < 2 * width:
                kv_ref[:, at - width : at - width + PAIR] = turn(piece, cos, low, high).astype(bf16)
            else:
                kv_ref[:, at - width : at - width + PAIR] = piece.astype(bf16)


def by_head(x):
    first = (lax.broadcasted_iota(jnp.int32, (1, PAIR), 1) < HEAD_DIM).astype(f32)
    return jnp.concatenate([x * first.astype(bf16), x * (1.0 - first).astype(bf16)], axis=0)


def own_heads(x):
    both = jnp.concatenate([x[:HEAD_DIM, :BLOCK], x[HEAD_DIM:, BLOCK:]], axis=0)
    return both.T


def fill(dst, left, mid, right):
    n = mid.shape[1]
    dst[0:WIN] = left[0]
    dst[WIN : WIN + n] = mid[0]
    dst[WIN + n : 2 * WIN + n] = right[0]


def attend_kernel(q_ref, k_ref, v_ref, lk_ref, lv_ref, rk_ref, rv_ref, bias_ref, att_ref, p_ref, ke, ve):
    fill(ke, lk_ref, k_ref, rk_ref)
    fill(ve, lv_ref, v_ref, rv_ref)
    vt = ve[...].T
    for i in range(q_ref.shape[1] // BLOCK):
        rows = slice(i * BLOCK, (i + 1) * BLOCK)
        span = slice(i * BLOCK, (i + 1) * BLOCK + 2 * WIN)
        scores = mm(ke[span], by_head(q_ref[0, rows]), NT)
        scores = scores + jnp.concatenate([bias_ref[i]] * 2, axis=1)
        raised = jnp.exp(scores - jnp.max(scores, axis=0, keepdims=True))
        total = jnp.sum(raised, axis=0, keepdims=True)
        probs = (raised * (1.0 / total)).astype(bf16)
        p_ref[0, 0, i] = probs
        att_ref[0, rows] = own_heads(mm(vt[:, span], probs)).astype(bf16)


def attend_back_kernel(
    q_ref, k_ref, v_ref, lk_ref, lv_ref, rk_ref, rv_ref, p_ref, ag_ref, cos_ref, low_ref, high_ref,
    dq_ref, dk_ref, dv_ref, dl_ref, dr_ref, ke, ve, ka, va,
):
    fill(ke, lk_ref, k_ref, rk_ref)
    fill(ve, lv_ref, v_ref, rv_ref)
    ka[...] = jnp.zeros_like(ka)
    va[...] = jnp.zeros_like(va)
    count = q_ref.shape[1]
    scale = 1.0 / math.sqrt(HEAD_DIM)
    kt = ke[...].T
    for i in range(count // BLOCK):
        rows = slice(i * BLOCK, (i + 1) * BLOCK)
        span = slice(i * BLOCK, (i + 1) * BLOCK + 2 * WIN)
        upstream = by_head(ag_ref[0, rows])
        low_probs = p_ref[0, 0, i]
        probs = low_probs.astype(f32)
        back = mm(ve[span], upstream, NT)
        delta = jnp.sum(probs * back, axis=0, keepdims=True)
        grad = (probs * (back - delta)).astype(bf16)
        dq = own_heads(mm(kt[:, span], grad)) * scale
        at = slice(WIN + i * BLOCK, WIN + (i + 1) * BLOCK)
        dq_ref[0, rows] = turn(dq, cos_ref[at], -low_ref[at], -high_ref[at]).astype(bf16)
        ka[span] += mm(grad, by_head(q_ref[0, rows]))
        va[span] += mm(low_probs, upstream)
    dk = turn(ka[...], cos_ref[...], -low_ref[...], -high_ref[...])
    dl_ref[0, 0] = dk[:WIN].astype(bf16)
    dk_ref[0] = dk[WIN : WIN + count].astype(bf16)
    dr_ref[0, 0] = dk[WIN + count :].astype(bf16)
    dl_ref[0, 1] = va[:WIN].astype(bf16)
    dv_ref[0] = va[WIN : WIN + count].astype(bf16)
    dr_ref[0, 1] = va[WIN + count :].astype(bf16)


def unpack(share, shapes):
    width = share.shape[1]
    outs, at = [], 0
    for n, columns in shapes:
        parts = []
        for _ in range(columns // width):
            parts.append(share[at : at + n])
            at += n
        outs.append(jnp.concatenate(parts, axis=1) if len(parts) > 1 else parts[0])
    return outs


def padded_rows(n, seq_size):
    unit = 16 * seq_size
    return -(-n // unit) * unit


def mlp_kernel(
    steps,
    tok_ref, att_ref, go_ref, gain_ref, wo_ref, win_ref, wout_ref,
    out_ref, mg_ref, ag_ref, pack_ref, dgain_ref,
    awo, awin, awout, wg_buf, hid_buf,
):
    step = pl.program_id(0)

    @pl.when(step == 0)
    def _():
        dgain_ref[...] = jnp.zeros_like(dgain_ref)

    attended, go = att_ref[...], go_ref[...]
    middle = tok_ref[...].astype(f32) + mm(attended, wo_ref[...])
    gain = gain_ref[...]
    unit, inverse = unit_rows(middle)
    normed = (unit * gain).astype(bf16)
    chunk = 384
    for c in range(FF // chunk):
        cols = slice(c * chunk, (c + 1) * chunk)
        gate = slice(FF + c * chunk, FF + (c + 1) * chunk)
        a = mm(normed, win_ref[:, cols])
        b = mm(normed, win_ref[:, gate])
        hg = mm(go, wout_ref[cols, :], NT)
        cdf = 0.5 * (1.0 + lax.erf(a * (1.0 / math.sqrt(2.0))))
        gelu = a * cdf
        slope = cdf + a * (jnp.exp(-0.5 * a * a) * (1.0 / math.sqrt(2.0 * math.pi)))
        hid_buf[:, cols] = (gelu * b).astype(bf16)
        wg_buf[:, cols] = (hg * b * slope).astype(bf16)
        wg_buf[:, gate] = (hg * gelu).astype(bf16)
    hidden, wg = hid_buf[...], wg_buf[...]
    out_ref[...] = (middle + mm(hidden, wout_ref[...])).astype(bf16)
    back = mm(wg, win_ref[...], NT)
    dgain_ref[...] += jnp.sum(back * unit, axis=0, keepdims=True)
    e = back * gain
    part = e - jnp.mean(e, axis=-1, keepdims=True) - unit * jnp.mean(e * unit, axis=-1, keepdims=True)
    mg = go.astype(f32) + inverse * part
    mg_ref[...] = mg
    low = mg.astype(bf16)
    ag_ref[...] = mm(low, wo_ref[...], NT).astype(bf16)
    products = ((awin, normed, wg), (awo, attended, low), (awout, hidden, go))
    last = steps - 1

    @pl.when(step == 0)
    def _():
        for acc, lhs, rhs in products:
            acc[...] = mm(lhs, rhs, TN)

    if steps > 2:

        @pl.when((step > 0) & (step < last))
        def _():
            for acc, lhs, rhs in products:
                acc[...] += mm(lhs, rhs, TN)

    @pl.when(step == last)
    def _():
        shares, depth, width = pack_ref.shape
        at = 0
        for acc, lhs, rhs in products:
            n = acc.shape[0] // shares
            for j in range(acc.shape[1] // width):
                cols = slice(j * width, (j + 1) * width)
                for f in range(shares):
                    mine = slice(f * n, (f + 1) * n)
                    piece = mm(lhs[:, mine], rhs[:, cols], TN) + acc[mine, cols]
                    pack_ref[f, at : at + n] = piece.astype(bf16)
                at += n
        if at < depth:
            for f in range(shares):
                pack_ref[f, at:] = jnp.zeros((depth - at, width), bf16)


def qkv_back_kernel(
    prior, kept, last, tok_ref, mg_ref, dq_ref, dk_ref, dv_ref, fl_ref, fr_ref, gain_ref, w_ref, *refs
):
    tg_ref, dw_ref, dgain_ref, buf = refs[prior + kept :]
    width = tok_ref.shape[2]
    count = tok_ref.shape[1]
    buf[:, :width] = dq_ref[0]
    for j, ref in enumerate((dk_ref, dv_ref)):
        cols = slice((j + 1) * width, (j + 2) * width)
        buf[:, cols] = ref[0]
        buf[:WIN, cols] = (ref[0, :WIN].astype(f32) + fl_ref[0, j].astype(f32)).astype(bf16)
        buf[count - WIN :, cols] = (
            ref[0, count - WIN :].astype(f32) + fr_ref[0, j].astype(f32)
        ).astype(bf16)
    gain = gain_ref[...]
    unit, inverse = unit_rows(tok_ref[0].astype(f32))
    normed = (unit * gain).astype(bf16)
    grads = buf[...]
    back = mm(grads, w_ref[...], NT)
    gain_grad = jnp.sum(back * unit, axis=0, keepdims=True)
    dgain_ref[...] = gain_grad + refs[1][...] if prior else gain_grad
    e = back * gain
    part = e - jnp.mean(e, axis=-1, keepdims=True) - unit * jnp.mean(e * unit, axis=-1, keepdims=True)
    tg_ref[0] = mg_ref[0] + inverse * part
    for j in range(3):
        cols = slice(j * width, (j + 1) * width)
        piece = mm(normed, grads[:, cols], TN)
        if prior:
            piece = piece + refs[0][:, cols].astype(f32)
        if not last:
            dw_ref[:, cols] = piece.astype(bf16)
            continue
        shares = dw_ref.shape[0]
        n = piece.shape[0] // shares
        for f in range(shares):
            dw_ref[f, j * n : (j + 1) * n] = piece[f * n : (f + 1) * n].astype(bf16)
    if last:
        at = 3 * w_ref.shape[0] // dw_ref.shape[0]
        dw_ref[:, at:] = jnp.zeros((dw_ref.shape[0], dw_ref.shape[1] - at, width), bf16)


def gather_plan(shapes):
    plan = []
    for a, (n, columns) in enumerate(shapes):
        half = n // 2
        parts = 2 if half % 32 == 0 and n * columns > 300000 else 1
        plan += [(a, k * half // parts, half // parts) for k in range(parts)]
    return plan


def gather_kernel(*refs):
    many = (len(refs) - 7) // 2
    ins, outs = refs[:many], refs[many : 2 * many]
    own_sem, xs, xr, ys, yr, cs, cr = refs[2 * many :]
    plan = gather_plan([r.shape for r in ins])
    count = len(plan)
    seq, me = lax.axis_index("seq"), lax.axis_index("fsdp")
    across = lax.rem(me + 2, 4)
    core = me + 1 - 2 * lax.rem(me, 2)
    side = lax.rem(seq, 2)
    beside = {"seq": seq + 1 - 2 * side}
    barrier = pltpu.get_barrier_semaphore()
    for target in ({"fsdp": across}, {"fsdp": core}, beside):
        pl.semaphore_signal(barrier, inc=1, device_id=target, device_id_type=pl.DeviceIdType.MESH)
    pl.semaphore_wait(barrier, 3)

    def send(src, dst, ss, rs, target):
        copy = pltpu.make_async_remote_copy(
            src_ref=src, dst_ref=dst, send_sem=ss, recv_sem=rs,
            device_id=target, device_id_type=pl.DeviceIdType.MESH,
        )
        copy.start()
        return copy

    def place(a, owner, which, off, n):
        rows = ins[a].shape[0]
        at = owner * rows + which * (rows // 2) + off
        return outs[a].at[pl.ds(pl.multiple_of(at, 16), n)]

    def first_hop(k):
        a, off, n = plan[k]
        half = ins[a].shape[0] // 2
        src = ins[a].at[pl.ds(pl.multiple_of(side * half + off, 16), n)]
        return send(src, place(a, me, side, off, n), xs.at[k], xr.at[k], {"fsdp": across})

    hops = [first_hop(k) for k in range(count)]
    local, pairs = [], []
    for a in range(many):
        n = ins[a].shape[0]
        spot = outs[a].at[pl.ds(pl.multiple_of(me * n, 16), n)]
        copy = pltpu.make_async_copy(ins[a], spot, own_sem.at[a])
        copy.start()
        local.append(copy)
        pairs.append(send(ins[a], spot, cs.at[a], cr.at[a], {"fsdp": core}))
    seconds = []

    def relay(k):
        a, off, n = plan[k]
        seconds[k].wait_recv()
        spot = place(a, across, 1 - side, off, n)
        i = many + count + k
        pairs.append(send(spot, spot, cs.at[i], cr.at[i], {"fsdp": core}))

    for k in range(count):
        a, off, n = plan[k]
        hops[k].wait_recv()
        spot = place(a, across, side, off, n)
        seconds.append(send(spot, spot, ys.at[k], yr.at[k], beside))
        pairs.append(send(spot, spot, cs.at[many + k], cr.at[many + k], {"fsdp": core}))
        if k:
            relay(k - 1)
    relay(count - 1)
    for copy in local:
        copy.wait()
    for copy in hops + seconds:
        copy.wait_send()
    for copy in pairs:
        copy.wait_send()
        copy.wait_recv()


def gather_weights(*weights):
    count, many = len(gather_plan([w.shape for w in weights])), len(weights)
    sems = lambda n: pltpu.SemaphoreType.DMA((n,))
    return pl.pallas_call(
        gather_kernel,
        in_specs=[pl.BlockSpec(memory_space=pl.ANY)] * many,
        out_specs=[pl.BlockSpec(memory_space=pl.ANY)] * many,
        out_shape=[sds((4 * w.shape[0], w.shape[1]), w.dtype) for w in weights],
        scratch_shapes=[sems(many)] + [sems(count)] * 4 + [sems(many + 2 * count)] * 2,
        compiler_params=pltpu.CompilerParams(collective_id=0, has_side_effects=True),
        cost_estimate=pl.CostEstimate(flops=0, bytes_accessed=2**26, transcendentals=0),
        name="gather_weights",
    )(*weights)


def reduce_kernel(seq_size, pack_ref, out_ref, mine, got, total, far, work, back, done, ls, cs, cr, xs, xr, ss, sr, gs, gr):
    me = lax.axis_index("fsdp")
    across = lax.rem(me + 2, 4)
    core = me + 1 - 2 * lax.rem(me, 2)
    barrier = pltpu.get_barrier_semaphore()
    seq = lax.axis_index("seq")
    hops_count = seq_size.bit_length() - 1
    bits = [lax.rem(lax.div(seq, 2**b), 2) for b in range(hops_count)]
    partners = [{"seq": seq + (1 - 2 * bits[b]) * 2**b} for b in range(hops_count)]
    for target in [{"fsdp": across}, {"fsdp": core}] + partners:
        pl.semaphore_signal(barrier, inc=1, device_id=target, device_id_type=pl.DeviceIdType.MESH)
    pl.semaphore_wait(barrier, 2 + hops_count)
    parts = xs.shape[0]
    lanes = out_ref.shape[1] // 2
    n = out_ref.shape[0] // parts
    rows = [pl.ds(k * n, n) for k in range(parts)]

    def send(src, dst, ss, rs, target):
        copy = pltpu.make_async_remote_copy(
            src_ref=src, dst_ref=dst, send_sem=ss, recv_sem=rs,
            device_id=target, device_id_type=pl.DeviceIdType.MESH,
        )
        copy.start()
        return copy

    pairs, locals_ = {}, {}
    for slot, theirs, ours in ((0, lax.rem(core + 2, 4), across), (1, core, me)):
        for k in range(parts):
            i = slot * parts + k
            pairs[slot, k] = send(pack_ref.at[theirs, rows[k]], got.at[slot, rows[k]], cs.at[i], cr.at[i], {"fsdp": core})
            copy = pltpu.make_async_copy(pack_ref.at[ours, rows[k]], mine.at[slot, rows[k]], ls.at[i])
            copy.start()
            locals_[slot, k] = copy
    hops = []
    for k in range(parts):
        locals_[0, k].wait()
        pairs[0, k].wait_recv()
        total[rows[k]] = (mine[0, rows[k]].astype(f32) + got[0, rows[k]].astype(f32)).astype(bf16)
        hops.append(send(total.at[rows[k]], far.at[rows[k]], xs.at[k], xr.at[k], {"fsdp": across}))
    for k in range(parts):
        locals_[1, k].wait()
        pairs[1, k].wait_recv()
        hops[k].wait_recv()
        share = (
            mine[1, rows[k]].astype(f32) + got[1, rows[k]].astype(f32) + far[rows[k]].astype(f32)
        ).astype(bf16)
        work[0, rows[k]] = share[:, :lanes]
        work[1, rows[k]] = share[:, lanes:]
    orders = [list(range(hops_count)), list(range(1, hops_count)) + [0]]
    low = [0, 0]
    size = out_ref.shape[0]
    offset = 0
    copies = []
    span = lambda at, n: pl.ds(pl.multiple_of(at, 16), n)
    for t in range(hops_count):
        size //= 2
        started = []
        for h in range(2):
            b = orders[h][t]
            spot = back.at[h, pl.ds(offset, size)]
            gone = work.at[h, span(low[h] + (1 - bits[b]) * size, size)]
            i = 2 * t + h
            started.append(send(gone, spot, ss.at[i], sr.at[i], partners[b]))
            low[h] = low[h] + bits[b] * size
        for h in range(2):
            started[h].wait_recv()
            here = span(low[h], size)
            value = work[h, here].astype(f32) + back[h, pl.ds(offset, size)].astype(f32)
            if t < hops_count - 1:
                work[h, here] = value.astype(bf16)
            else:
                done[h, here] = value.astype(bf16)
        copies += started
        offset += size
    for t in reversed(range(hops_count)):
        started = []
        for h in range(2):
            b = orders[h][t]
            here = done.at[h, span(low[h], size)]
            i = 2 * t + h
            started.append(send(here, here, gs.at[i], gr.at[i], partners[b]))
        for h in range(2):
            started[h].wait_recv()
            low[h] = low[h] - bits[orders[h][t]] * size
        copies += started
        size *= 2
    for copy in list(pairs.values()) + hops + copies:
        copy.wait_send()
    out_ref[:, :lanes] = done[0]
    out_ref[:, lanes:] = done[1]


def reduce_all(x, parts, seq_size):
    shares, n, width = x.shape
    sems = lambda m: pltpu.SemaphoreType.DMA((m,))
    vmem = lambda *shape: pltpu.VMEM(shape, bf16)
    hops = 2 * (seq_size.bit_length() - 1)
    return pl.pallas_call(
        functools.partial(reduce_kernel, seq_size),
        in_specs=[pl.BlockSpec(memory_space=pl.ANY)],
        out_specs=pl.BlockSpec(memory_space=pltpu.VMEM),
        out_shape=sds((n, width), bf16),
        scratch_shapes=[vmem(2, n, width), vmem(2, n, width), vmem(n, width), vmem(n, width)]
        + [vmem(2, n, width // 2)] * 3
        + [sems(2 * parts)] * 3 + [sems(parts)] * 2 + [sems(hops)] * 4,
        compiler_params=pltpu.CompilerParams(collective_id=1, has_side_effects=True, vmem_limit_bytes=LIMIT),
        cost_estimate=pl.CostEstimate(flops=0, bytes_accessed=2**26, transcendentals=0),
        name="reduce_all",
    )(x)


def sds(shape, dtype):
    return jax.ShapeDtypeStruct(shape, dtype)


def whole(shape):
    return pl.BlockSpec(shape, lambda *_: (0,) * len(shape), pipeline_mode=pl.Buffered(1))


def tables(start, count):
    half = HEAD_DIM // 2
    freqs = rope_base ** (-(jnp.arange(half, dtype=f32) * 2.0 / HEAD_DIM))
    positions = (start + jnp.arange(count, dtype=jnp.int32)).astype(f32)
    angles = positions[:, None] * freqs[None, :]
    cos, sin = jnp.cos(angles), jnp.sin(angles)
    none = jnp.zeros_like(sin)
    return (
        jnp.concatenate([cos] * 4, axis=-1),
        jnp.concatenate([-sin, none] * 2, axis=-1),
        jnp.concatenate([none, sin] * 2, axis=-1),
    )


def shards(tokens, norm_gain_attn, qkv_weight, attn_out_weight, norm_gain_mlp, mlp_in_weight, mlp_out_weight, grad_out):
    seqs, piece, width = tokens.shape
    rows = seqs * piece
    span = piece + 2 * WIN
    pairs = width // PAIR
    seq_size = lax.axis_size("seq")
    shares = lax.axis_size("fsdp")
    mlp_shapes = (mlp_in_weight.shape, attn_out_weight.shape, mlp_out_weight.shape)
    mlp_rows = sum(n * m // width for n, m in mlp_shapes)
    qkv_rows = padded_rows(3 * qkv_weight.shape[0] + 16, seq_size)
    forward = [(i, i + 1) for i in range(seq_size - 1)]
    backward = [(j, i) for i, j in forward]
    gather = lambda x: lax.all_gather(x, "fsdp", axis=0, tiled=True)
    gains = jnp.stack([norm_gain_attn, norm_gain_mlp])
    own_gains = gains.shape[1]
    gains = jnp.pad(gains, ((0, 30), (0, -own_gains % PAIR)))
    w_qkv, gains = gather_weights(qkv_weight, gains)
    gains = gains.reshape(shares, 32, -1)[:, :2, :own_gains].swapaxes(0, 1).reshape(2, width)
    w_attn = gather(attn_out_weight)
    w_in = gather(mlp_in_weight)
    w_out = gather(mlp_out_weight)
    gain_attn = gains[0:1].astype(f32)
    gain_mlp = gains[1:2].astype(f32)
    start = lax.axis_index("seq") * piece
    cos, low, high = tables(start - WIN, span)
    q_at = start + jnp.arange(piece, dtype=jnp.int32).reshape(-1, BLOCK)[:, None, :]
    k_at = (
        start - WIN
        + jnp.arange(piece // BLOCK, dtype=jnp.int32)[:, None, None] * BLOCK
        + jnp.arange(BLOCK + 2 * WIN, dtype=jnp.int32)[None, :, None]
    )
    inside = (jnp.abs(q_at - k_at) <= WIN) & (k_at >= 0) & (k_at < piece * seq_size)
    bias = jnp.where(inside, 0.0, negative).astype(f32)

    tile = 256
    per = piece // tile
    flat = lambda x: x.reshape(rows, x.shape[-1])
    row_spec = lambda w: pl.BlockSpec((tile, w), lambda i: (i, 0))
    table_spec = pl.BlockSpec((tile, PAIR), lambda i: (lax.rem(i, per), 0))
    params = lambda n: pltpu.CompilerParams(dimension_semantics=("arbitrary",) * n, vmem_limit_bytes=LIMIT)
    tok = flat(tokens)
    mid = slice(WIN, WIN + piece)
    def project(x, *rotary):
        count = x.shape[0]
        return pl.pallas_call(
            qkv_kernel,
            grid=(count // tile,),
            in_specs=[row_spec(width), whole((1, width)), whole(w_qkv.shape), table_spec, table_spec, table_spec],
            out_specs=[row_spec(width), row_spec(2 * width)],
            out_shape=[sds((count, width), bf16), sds((count, 2 * width), bf16)],
            compiler_params=params(1),
            cost_estimate=pl.CostEstimate(flops=6 * count * width * width, bytes_accessed=12 * count * width, transcendentals=0),
            name="qkv_forward",
        )(x, gain_attn, w_qkv, *rotary)

    borders = lambda x, n: jnp.concatenate([x[..., :WIN, :], x[..., n - WIN :, :]], axis=-2)
    _, kv_border = project(
        borders(tokens, piece).reshape(-1, width),
        *(jnp.tile(borders(t[mid], piece), (seqs, 1)) for t in (cos, low, high)),
    )
    kv_border = kv_border.reshape(seqs, 2 * WIN, 2 * width)
    left = lax.ppermute(kv_border[:, WIN:], "seq", forward)
    right = lax.ppermute(kv_border[:, :WIN], "seq", backward)
    q, kv = project(tok, cos[mid], low[mid], high[mid])
    q = q.reshape(seqs, piece, width)
    kv = kv.reshape(seqs, piece, 2 * width)

    def lanes(n, off=0):
        return pl.BlockSpec((1, n, PAIR), lambda s, p: (s, 0, p + off))

    kv_specs = [
        lanes(piece), lanes(piece, pairs), lanes(WIN), lanes(WIN, pairs), lanes(WIN), lanes(WIN, pairs),
    ]
    kv_args = (kv, kv, left, left, right, right)
    p_block = (1, 1, piece // BLOCK, BLOCK + 2 * WIN, 2 * BLOCK)
    p_spec = pl.BlockSpec(p_block, lambda s, p: (s, p, 0, 0, 0))
    p_shape = (seqs, pairs) + p_block[2:]
    ext = pltpu.VMEM((span, PAIR), bf16)
    unit_flops = 2 * seqs * HEADS * piece * (BLOCK + 2 * WIN) * HEAD_DIM
    p_bytes = 2 * math.prod(p_shape)
    attended, probs = pl.pallas_call(
        attend_kernel,
        grid=(seqs, pairs),
        in_specs=[lanes(piece)] + kv_specs + [whole(bias.shape)],
        out_specs=[lanes(piece), p_spec],
        out_shape=[sds((seqs, piece, width), bf16), sds(p_shape, bf16)],
        scratch_shapes=[ext, ext],
        compiler_params=params(2),
        cost_estimate=pl.CostEstimate(flops=8 * unit_flops, bytes_accessed=p_bytes + 8 * rows * width, transcendentals=p_bytes // 2),
        name="attend_forward",
    )(q, *kv_args, bias)

    wide = piece
    wide_spec = pl.BlockSpec((wide, width), lambda i: (i, 0))
    out, mg, ag, d_mlp, d_gain_mlp = pl.pallas_call(
        functools.partial(mlp_kernel, rows // wide),
        grid=(rows // wide,),
        in_specs=[wide_spec] * 3 + [whole((1, width)), whole(w_attn.shape), whole(w_in.shape), whole(w_out.shape)],
        out_specs=[wide_spec] * 3
        + [whole((shares, mlp_rows, width)), whole((1, width))],
        out_shape=[
            sds((rows, width), bf16), sds((rows, width), f32), sds((rows, width), bf16),
            sds((shares, mlp_rows, width), bf16), sds((1, width), f32),
        ],
        scratch_shapes=[
            pltpu.VMEM(w_attn.shape, f32), pltpu.VMEM(w_in.shape, f32), pltpu.VMEM(w_out.shape, f32),
            pltpu.VMEM((wide, 2 * FF), bf16), pltpu.VMEM((wide, FF), bf16),
        ],
        compiler_params=params(1),
        cost_estimate=pl.CostEstimate(flops=6 * rows * width * (width + 3 * FF), bytes_accessed=40 * 2**20, transcendentals=0),
        name="mlp_both_ways",
    )(tok, flat(attended), flat(grad_out), gain_mlp, w_attn, w_in, w_out)

    mlp_sum = lax.psum(lax.psum_scatter(d_mlp, "fsdp", scatter_dimension=0, tiled=True)[0], "seq")

    table_full = pl.BlockSpec((span, PAIR), lambda p: (0, 0))
    edge_shape = sds((1, 2, WIN, width), bf16)
    own = sds((1, piece, width), bf16)
    total = pltpu.VMEM((span, PAIR), f32)
    ag = ag.reshape(seqs, piece, width)
    mg = mg.reshape(seqs, piece, width)

    def attend_back(s):
        def at(n, off=0):
            return pl.BlockSpec((1, n, PAIR), lambda p: (s, 0, p + off))

        here = pl.BlockSpec((1, piece, PAIR), lambda p: (0, 0, p))
        edge = pl.BlockSpec((1, 2, WIN, PAIR), lambda p: (0, 0, 0, p))
        return pl.pallas_call(
            attend_back_kernel,
            grid=(pairs,),
            in_specs=[at(piece), at(piece), at(piece, pairs), at(WIN), at(WIN, pairs), at(WIN), at(WIN, pairs)]
            + [pl.BlockSpec(p_block, lambda p: (s, p, 0, 0, 0)), at(piece)]
            + [table_full] * 3,
            out_specs=[here] * 3 + [edge, edge],
            out_shape=[own] * 3 + [edge_shape] * 2,
            scratch_shapes=[ext, ext, total, total],
            compiler_params=params(1),
            cost_estimate=pl.CostEstimate(flops=8 * unit_flops, bytes_accessed=p_bytes // 2 + 8 * rows * width, transcendentals=0),
            name="attend_backward",
        )(q, *kv_args, probs, ag, cos, low, high)

    one = pl.BlockSpec((1, piece, width), lambda i: (0, 0, 0))
    edge_in = pl.BlockSpec((1, 2, WIN, width), lambda i: (0, 0, 0, 0))

    def qkv_back(s, grads, before, tokens_grad):
        this = pl.BlockSpec((1, piece, width), lambda i: (s, 0, 0))
        last = s == seqs - 1
        prior = [] if before is None else list(before)
        to = (shares, qkv_rows, width) if last else w_qkv.shape
        kept = [] if tokens_grad is None else [tokens_grad]
        args = [tokens, mg, *grads, gain_attn, w_qkv, *prior, *kept]
        return pl.pallas_call(
            functools.partial(qkv_back_kernel, len(prior), len(kept), last),
            grid=(1,),
            in_specs=[this] * 2 + [one] * 3 + [edge_in] * 2 + [whole((1, width)), whole(w_qkv.shape)]
            + [whole(p.shape) for p in prior] + [pl.BlockSpec(memory_space=pl.ANY)] * len(kept),
            out_specs=[this, whole(to), whole((1, width))],
            out_shape=[sds(tokens.shape, f32), sds(to, bf16), sds((1, width), f32)],
            scratch_shapes=[pltpu.VMEM((piece, 3 * width), bf16)],
            input_output_aliases={len(args) - 1: 0} if kept else {},
            compiler_params=params(1),
            cost_estimate=pl.CostEstimate(flops=12 * piece * width * width, bytes_accessed=20 * piece * width, transcendentals=0),
            name="qkv_backward",
        )(*args)

    grads = []
    for s in range(seqs):
        dq, dk, dv, dl, dr = attend_back(s)
        grads.append((dq, dk, dv, lax.ppermute(dr, "seq", forward), lax.ppermute(dl, "seq", backward)))
    before = tokens_grad = None
    for s in range(seqs):
        tokens_grad, *before = qkv_back(s, grads[s], before, tokens_grad)
    d_wqkv, d_gain_attn = before

    gains_at = 3 * qkv_weight.shape[0]
    both = jnp.concatenate([d_gain_attn, d_gain_mlp]).astype(bf16)
    both = both.reshape(2, shares, width // shares).swapaxes(0, 1)
    both = jnp.pad(both, ((0, 0), (0, 0), (0, width - width // shares)))
    d_wqkv = lax.dynamic_update_slice(d_wqkv, both, (0, gains_at, 0))
    qkv_sum = reduce_all(d_wqkv, 4, seq_size)
    s_wqkv = unpack(qkv_sum, (qkv_weight.shape,))[0]
    s_gains = qkv_sum[gains_at : gains_at + 2, : width // shares].astype(f32)
    s_win, s_wo, s_wout = unpack(mlp_sum, mlp_shapes)
    return (
        out.reshape(seqs, piece, width),
        tokens_grad,
        s_gains[0],
        s_wqkv.astype(f32),
        s_wo.astype(f32),
        s_gains[1],
        s_win.astype(f32),
        s_wout.astype(f32),
    )


def solution(mesh):
    return jax.shard_map(
        shards,
        mesh=mesh,
        in_specs=(
            P("fsdp", "seq", None),
            P("fsdp"),
            P("fsdp", None),
            P("fsdp", None),
            P("fsdp"),
            P("fsdp", None),
            P("fsdp", None),
            P("fsdp", "seq", None),
        ),
        out_specs=(
            P("fsdp", "seq", None),
            P("fsdp", "seq", None),
            P("fsdp"),
            P("fsdp", None),
            P("fsdp", None),
            P("fsdp"),
            P("fsdp", None),
            P("fsdp", None),
        ),
        check_vma=False,
    )
```

```python
import functools
import math

import jax
import jax.numpy as jnp
from jax import lax
from jax.experimental import pallas as pl
from jax.experimental.pallas import tpu as pltpu
from jax.sharding import PartitionSpec as P

HEADS = 12
HEAD_DIM = 64
FF = 1152
WIN = 64
PAIR = 128
BLOCK = 64

epsilon = 1e-05
rope_base = 10000.0
negative = -1e30
f32 = jnp.float32
bf16 = jnp.bfloat16
LIMIT = 56 * 1024 * 1024

NN = (((1,), (0,)), ((), ()))
NT = (((1,), (1,)), ((), ()))
TN = (((0,), (0,)), ((), ()))


def mm(a, b, dims=NN):
    return lax.dot_general(a, b, dims, preferred_element_type=f32)


def unit_rows(x):
    center = x - jnp.mean(x, axis=-1, keepdims=True)
    inverse = lax.rsqrt(jnp.mean(center * center, axis=-1, keepdims=True) + epsilon)
    return center * inverse, inverse


def turn(x, cos, low, high):
    return x * cos + pltpu.roll(x, PAIR - 32, 1) * low + pltpu.roll(x, 32, 1) * high


def qkv_kernel(tok_ref, gain_ref, w_ref, cos_ref, low_ref, high_ref, q_ref, kv_ref):
    unit, _ = unit_rows(tok_ref[...].astype(f32))
    normed = (unit * gain_ref[...]).astype(bf16)
    cos, low, high = cos_ref[...], low_ref[...], high_ref[...]
    width = q_ref.shape[1]
    step = 2 * PAIR
    for j in range(3 * width // step):
        part = mm(normed, w_ref[:, j * step : (j + 1) * step])
        for h in range(2):
            at = j * step + h * PAIR
            piece = part[:, h * PAIR : (h + 1) * PAIR]
            if at < width:
                q_ref[:, at : at + PAIR] = (
                    turn(piece, cos, low, high) * (1.0 / math.sqrt(HEAD_DIM))
                ).astype(bf16)
            elif at < 2 * width:
                kv_ref[:, at - width : at - width + PAIR] = turn(piece, cos, low, high).astype(bf16)
            else:
                kv_ref[:, at - width : at - width + PAIR] = piece.astype(bf16)


def by_head(x):
    first = (lax.broadcasted_iota(jnp.int32, (1, PAIR), 1) < HEAD_DIM).astype(f32)
    return jnp.concatenate([x * first.astype(bf16), x * (1.0 - first).astype(bf16)], axis=0)


def own_heads(x):
    turned = x.T
    first = lax.broadcasted_iota(jnp.int32, (1, PAIR), 1) < HEAD_DIM
    return jnp.where(first, turned[:BLOCK], turned[BLOCK:])


def columns(x):
    return x.T, x[BLOCK:].T


def span_of(pair, i):
    at = (i - i % 2) * BLOCK
    return pair[i % 2][:, at : at + BLOCK + 2 * WIN]


def fill(dst, left, mid, right):
    n = mid.shape[1]
    dst[0:WIN] = left[0]
    dst[WIN : WIN + n] = mid[0]
    dst[WIN + n : 2 * WIN + n] = right[0]


def attend_kernel(q_ref, k_ref, v_ref, lk_ref, lv_ref, rk_ref, rv_ref, bias_ref, att_ref, p_ref, ke, ve):
    fill(ke, lk_ref, k_ref, rk_ref)
    fill(ve, lv_ref, v_ref, rv_ref)
    vt = columns(ve[...])
    for i in range(q_ref.shape[1] // BLOCK):
        rows = slice(i * BLOCK, (i + 1) * BLOCK)
        span = slice(i * BLOCK, (i + 1) * BLOCK + 2 * WIN)
        scores = mm(ke[span], by_head(q_ref[0, rows]), NT)
        scores = scores + bias_ref[i]
        raised = jnp.exp(scores - jnp.max(scores, axis=0, keepdims=True))
        total = jnp.sum(raised, axis=0, keepdims=True)
        probs = (raised * (1.0 / total)).astype(bf16)
        p_ref[0, 0, i] = probs
        att_ref[0, rows] = own_heads(mm(span_of(vt, i), probs)).astype(bf16)


def attend_back_kernel(
    q_ref, k_ref, v_ref, lk_ref, lv_ref, rk_ref, rv_ref, p_ref, ag_ref, cos_ref, low_ref, high_ref,
    dq_ref, dk_ref, dv_ref, dl_ref, dr_ref, ke, ve, ka, va,
):
    fill(ke, lk_ref, k_ref, rk_ref)
    fill(ve, lv_ref, v_ref, rv_ref)
    ka[...] = jnp.zeros_like(ka)
    va[...] = jnp.zeros_like(va)
    count = q_ref.shape[1]
    scale = 1.0 / math.sqrt(HEAD_DIM)
    kt = columns(ke[...])
    for i in range(count // BLOCK):
        rows = slice(i * BLOCK, (i + 1) * BLOCK)
        span = slice(i * BLOCK, (i + 1) * BLOCK + 2 * WIN)
        upstream = by_head(ag_ref[0, rows])
        low_probs = p_ref[0, 0, i]
        probs = low_probs.astype(f32)
        back = mm(ve[span], upstream, NT)
        delta = jnp.sum(probs * back, axis=0, keepdims=True)
        grad = (probs * (back - delta)).astype(bf16)
        dq = own_heads(mm(span_of(kt, i), grad)) * scale
        at = slice(WIN + i * BLOCK, WIN + (i + 1) * BLOCK)
        dq_ref[0, rows] = turn(dq, cos_ref[at], -low_ref[at], -high_ref[at]).astype(bf16)
        ka[span] += mm(grad, by_head(q_ref[0, rows]))
        va[span] += mm(low_probs, upstream)
    dk = turn(ka[...], cos_ref[...], -low_ref[...], -high_ref[...])
    dl_ref[0, 0] = dk[:WIN].astype(bf16)
    dk_ref[0] = dk[WIN : WIN + count].astype(bf16)
    dr_ref[0, 0] = dk[WIN + count :].astype(bf16)
    dl_ref[0, 1] = va[:WIN].astype(bf16)
    dv_ref[0] = va[WIN : WIN + count].astype(bf16)
    dr_ref[0, 1] = va[WIN + count :].astype(bf16)


def unpack(share, shapes):
    width = share.shape[1]
    outs, at = [], 0
    for n, columns in shapes:
        parts = []
        for _ in range(columns // width):
            parts.append(share[at : at + n])
            at += n
        outs.append(jnp.concatenate(parts, axis=1) if len(parts) > 1 else parts[0])
    return outs


def padded_rows(n, seq_size):
    unit = 16 * seq_size
    return -(-n // unit) * unit


def mlp_kernel(
    steps,
    tok_ref, att_ref, go_ref, gain_ref, wo_ref, win_ref, wout_ref,
    out_ref, mg_ref, ag_ref, pack_ref, dgain_ref,
    awo, awin, awout, wg_buf, hid_buf,
):
    step = pl.program_id(0)

    @pl.when(step == 0)
    def _():
        dgain_ref[...] = jnp.zeros_like(dgain_ref)

    attended, go = att_ref[...], go_ref[...]
    middle = tok_ref[...].astype(f32) + mm(attended, wo_ref[...])
    gain = gain_ref[...]
    unit, inverse = unit_rows(middle)
    normed = (unit * gain).astype(bf16)
    chunk = 384
    for c in range(FF // chunk):
        cols = slice(c * chunk, (c + 1) * chunk)
        gate = slice(FF + c * chunk, FF + (c + 1) * chunk)
        a = mm(normed, win_ref[:, cols])
        b = mm(normed, win_ref[:, gate])
        hg = mm(go, wout_ref[cols, :], NT)
        cdf = 0.5 * (1.0 + lax.erf(a * (1.0 / math.sqrt(2.0))))
        gelu = a * cdf
        slope = cdf + a * (jnp.exp(-0.5 * a * a) * (1.0 / math.sqrt(2.0 * math.pi)))
        hid_buf[:, cols] = (gelu * b).astype(bf16)
        wg_buf[:, cols] = (hg * b * slope).astype(bf16)
        wg_buf[:, gate] = (hg * gelu).astype(bf16)
    hidden, wg = hid_buf[...], wg_buf[...]
    out_ref[...] = (middle + mm(hidden, wout_ref[...])).astype(bf16)
    back = mm(wg, win_ref[...], NT)
    dgain_ref[...] += jnp.sum(back * unit, axis=0, keepdims=True)
    e = back * gain
    part = e - jnp.mean(e, axis=-1, keepdims=True) - unit * jnp.mean(e * unit, axis=-1, keepdims=True)
    mg = go.astype(f32) + inverse * part
    mg_ref[...] = mg
    low = mg.astype(bf16)
    ag_ref[...] = mm(low, wo_ref[...], NT).astype(bf16)
    products = ((awin, normed, wg), (awo, attended, low), (awout, hidden, go))
    last = steps - 1

    @pl.when(step == 0)
    def _():
        for acc, lhs, rhs in products:
            acc[...] = mm(lhs, rhs, TN)

    if steps > 2:

        @pl.when((step > 0) & (step < last))
        def _():
            for acc, lhs, rhs in products:
                acc[...] += mm(lhs, rhs, TN)

    @pl.when(step == last)
    def _():
        shares, depth, width = pack_ref.shape
        at = 0
        for acc, lhs, rhs in products:
            n = acc.shape[0] // shares
            for j in range(acc.shape[1] // width):
                cols = slice(j * width, (j + 1) * width)
                for f in range(shares):
                    mine = slice(f * n, (f + 1) * n)
                    piece = mm(lhs[:, mine], rhs[:, cols], TN) + acc[mine, cols]
                    pack_ref[f, at : at + n] = piece.astype(bf16)
                at += n
        if at < depth:
            for f in range(shares):
                pack_ref[f, at:] = jnp.zeros((depth - at, width), bf16)


def qkv_back_kernel(
    prior, kept, last, tok_ref, mg_ref, dq_ref, dk_ref, dv_ref, fl_ref, fr_ref, gain_ref, w_ref, *refs
):
    tg_ref, dw_ref, dgain_ref, buf = refs[prior + kept :]
    width = tok_ref.shape[2]
    count = tok_ref.shape[1]
    buf[:, :width] = dq_ref[0]
    for j, ref in enumerate((dk_ref, dv_ref)):
        cols = slice((j + 1) * width, (j + 2) * width)
        buf[:, cols] = ref[0]
        buf[:WIN, cols] = (ref[0, :WIN].astype(f32) + fl_ref[0, j].astype(f32)).astype(bf16)
        buf[count - WIN :, cols] = (
            ref[0, count - WIN :].astype(f32) + fr_ref[0, j].astype(f32)
        ).astype(bf16)
    gain = gain_ref[...]
    unit, inverse = unit_rows(tok_ref[0].astype(f32))
    normed = (unit * gain).astype(bf16)
    grads = buf[...]
    back = mm(grads, w_ref[...], NT)
    gain_grad = jnp.sum(back * unit, axis=0, keepdims=True)
    dgain_ref[...] = gain_grad + refs[1][...] if prior else gain_grad
    e = back * gain
    part = e - jnp.mean(e, axis=-1, keepdims=True) - unit * jnp.mean(e * unit, axis=-1, keepdims=True)
    tg_ref[0] = mg_ref[0] + inverse * part
    for j in range(3):
        cols = slice(j * width, (j + 1) * width)
        piece = mm(normed, grads[:, cols], TN)
        if prior:
            piece = piece + refs[0][:, cols].astype(f32)
        if not last:
            dw_ref[:, cols] = piece.astype(bf16)
            continue
        shares = dw_ref.shape[0]
        n = piece.shape[0] // shares
        for f in range(shares):
            dw_ref[f, j * n : (j + 1) * n] = piece[f * n : (f + 1) * n].astype(bf16)
    if last:
        at = 3 * w_ref.shape[0] // dw_ref.shape[0]
        dw_ref[:, at:] = jnp.zeros((dw_ref.shape[0], dw_ref.shape[1] - at, width), bf16)


def gather_plan(shapes):
    plan = []
    for a, (n, columns) in enumerate(shapes):
        half = n // 2
        parts = 2 if half % 32 == 0 and n * columns > 300000 else 1
        plan += [(a, k * half // parts, half // parts) for k in range(parts)]
    return plan


def gather_kernel(*refs):
    many = (len(refs) - 7) // 2
    ins, outs = refs[:many], refs[many : 2 * many]
    own_sem, xs, xr, ys, yr, cs, cr = refs[2 * many :]
    plan = gather_plan([r.shape for r in ins])
    count = len(plan)
    seq, me = lax.axis_index("seq"), lax.axis_index("fsdp")
    across = lax.rem(me + 2, 4)
    core = me + 1 - 2 * lax.rem(me, 2)
    side = lax.rem(seq, 2)
    beside = {"seq": seq + 1 - 2 * side}
    barrier = pltpu.get_barrier_semaphore()
    for target in ({"fsdp": across}, {"fsdp": core}, beside):
        pl.semaphore_signal(barrier, inc=1, device_id=target, device_id_type=pl.DeviceIdType.MESH)
    pl.semaphore_wait(barrier, 3)

    def send(src, dst, ss, rs, target):
        copy = pltpu.make_async_remote_copy(
            src_ref=src, dst_ref=dst, send_sem=ss, recv_sem=rs,
            device_id=target, device_id_type=pl.DeviceIdType.MESH,
        )
        copy.start()
        return copy

    def place(a, owner, which, off, n):
        rows = ins[a].shape[0]
        at = owner * rows + which * (rows // 2) + off
        return outs[a].at[pl.ds(pl.multiple_of(at, 16), n)]

    def first_hop(k):
        a, off, n = plan[k]
        half = ins[a].shape[0] // 2
        src = ins[a].at[pl.ds(pl.multiple_of(side * half + off, 16), n)]
        return send(src, place(a, me, side, off, n), xs.at[k], xr.at[k], {"fsdp": across})

    hops = [first_hop(k) for k in range(count)]
    local, pairs = [], []
    for a in range(many):
        n = ins[a].shape[0]
        spot = outs[a].at[pl.ds(pl.multiple_of(me * n, 16), n)]
        copy = pltpu.make_async_copy(ins[a], spot, own_sem.at[a])
        copy.start()
        local.append(copy)
        pairs.append(send(ins[a], spot, cs.at[a], cr.at[a], {"fsdp": core}))
    seconds = []

    def relay(k):
        a, off, n = plan[k]
        seconds[k].wait_recv()
        spot = place(a, across, 1 - side, off, n)
        i = many + count + k
        pairs.append(send(spot, spot, cs.at[i], cr.at[i], {"fsdp": core}))

    for k in range(count):
        a, off, n = plan[k]
        hops[k].wait_recv()
        spot = place(a, across, side, off, n)
        seconds.append(send(spot, spot, ys.at[k], yr.at[k], beside))
        pairs.append(send(spot, spot, cs.at[many + k], cr.at[many + k], {"fsdp": core}))
        if k:
            relay(k - 1)
    relay(count - 1)
    for copy in local:
        copy.wait()
    for copy in hops + seconds:
        copy.wait_send()
    for copy in pairs:
        copy.wait_send()
        copy.wait_recv()


def gather_weights(*weights):
    count, many = len(gather_plan([w.shape for w in weights])), len(weights)
    sems = lambda n: pltpu.SemaphoreType.DMA((n,))
    return pl.pallas_call(
        gather_kernel,
        in_specs=[pl.BlockSpec(memory_space=pl.ANY)] * many,
        out_specs=[pl.BlockSpec(memory_space=pl.ANY)] * many,
        out_shape=[sds((4 * w.shape[0], w.shape[1]), w.dtype) for w in weights],
        scratch_shapes=[sems(many)] + [sems(count)] * 4 + [sems(many + 2 * count)] * 2,
        compiler_params=pltpu.CompilerParams(collective_id=0, has_side_effects=True),
        cost_estimate=pl.CostEstimate(flops=0, bytes_accessed=2**26, transcendentals=0),
        name="gather_weights",
    )(*weights)


def reduce_kernel(seq_size, pack_ref, out_ref, mine, got, total, far, work, back, done, ls, cs, cr, xs, xr, ss, sr, gs, gr):
    me = lax.axis_index("fsdp")
    across = lax.rem(me + 2, 4)
    core = me + 1 - 2 * lax.rem(me, 2)
    barrier = pltpu.get_barrier_semaphore()
    seq = lax.axis_index("seq")
    hops_count = seq_size.bit_length() - 1
    bits = [lax.rem(lax.div(seq, 2**b), 2) for b in range(hops_count)]
    partners = [{"seq": seq + (1 - 2 * bits[b]) * 2**b} for b in range(hops_count)]
    for target in [{"fsdp": across}, {"fsdp": core}] + partners:
        pl.semaphore_signal(barrier, inc=1, device_id=target, device_id_type=pl.DeviceIdType.MESH)
    pl.semaphore_wait(barrier, 2 + hops_count)
    parts = xs.shape[0]
    lanes = out_ref.shape[1] // 2
    n = out_ref.shape[0] // parts
    rows = [pl.ds(k * n, n) for k in range(parts)]

    def send(src, dst, ss, rs, target):
        copy = pltpu.make_async_remote_copy(
            src_ref=src, dst_ref=dst, send_sem=ss, recv_sem=rs,
            device_id=target, device_id_type=pl.DeviceIdType.MESH,
        )
        copy.start()
        return copy

    pairs, locals_ = {}, {}
    for slot, theirs, ours in ((0, lax.rem(core + 2, 4), across), (1, core, me)):
        for k in range(parts):
            i = slot * parts + k
            pairs[slot, k] = send(pack_ref.at[theirs, rows[k]], got.at[slot, rows[k]], cs.at[i], cr.at[i], {"fsdp": core})
            copy = pltpu.make_async_copy(pack_ref.at[ours, rows[k]], mine.at[slot, rows[k]], ls.at[i])
            copy.start()
            locals_[slot, k] = copy
    hops = []
    for k in range(parts):
        locals_[0, k].wait()
        pairs[0, k].wait_recv()
        total[rows[k]] = (mine[0, rows[k]].astype(f32) + got[0, rows[k]].astype(f32)).astype(bf16)
        hops.append(send(total.at[rows[k]], far.at[rows[k]], xs.at[k], xr.at[k], {"fsdp": across}))
    for k in range(parts):
        locals_[1, k].wait()
        pairs[1, k].wait_recv()
        hops[k].wait_recv()
        share = (
            mine[1, rows[k]].astype(f32) + got[1, rows[k]].astype(f32) + far[rows[k]].astype(f32)
        ).astype(bf16)
        work[0, rows[k]] = share[:, :lanes]
        work[1, rows[k]] = share[:, lanes:]
    orders = [list(range(hops_count)), list(range(1, hops_count)) + [0]]
    low = [0, 0]
    size = out_ref.shape[0]
    offset = 0
    copies = []
    span = lambda at, n: pl.ds(pl.multiple_of(at, 16), n)
    for t in range(hops_count):
        size //= 2
        started = []
        for h in range(2):
            b = orders[h][t]
            spot = back.at[h, pl.ds(offset, size)]
            gone = work.at[h, span(low[h] + (1 - bits[b]) * size, size)]
            i = 2 * t + h
            started.append(send(gone, spot, ss.at[i], sr.at[i], partners[b]))
            low[h] = low[h] + bits[b] * size
        for h in range(2):
            started[h].wait_recv()
            here = span(low[h], size)
            value = work[h, here].astype(f32) + back[h, pl.ds(offset, size)].astype(f32)
            if t < hops_count - 1:
                work[h, here] = value.astype(bf16)
            else:
                done[h, here] = value.astype(bf16)
        copies += started
        offset += size
    for t in reversed(range(hops_count)):
        started = []
        for h in range(2):
            b = orders[h][t]
            here = done.at[h, span(low[h], size)]
            i = 2 * t + h
            started.append(send(here, here, gs.at[i], gr.at[i], partners[b]))
        for h in range(2):
            started[h].wait_recv()
            low[h] = low[h] - bits[orders[h][t]] * size
        copies += started
        size *= 2
    for copy in list(pairs.values()) + hops + copies:
        copy.wait_send()
    out_ref[:, :lanes] = done[0]
    out_ref[:, lanes:] = done[1]


def reduce_all(x, parts, seq_size):
    shares, n, width = x.shape
    sems = lambda m: pltpu.SemaphoreType.DMA((m,))
    vmem = lambda *shape: pltpu.VMEM(shape, bf16)
    hops = 2 * (seq_size.bit_length() - 1)
    return pl.pallas_call(
        functools.partial(reduce_kernel, seq_size),
        in_specs=[pl.BlockSpec(memory_space=pl.ANY)],
        out_specs=pl.BlockSpec(memory_space=pltpu.VMEM),
        out_shape=sds((n, width), bf16),
        scratch_shapes=[vmem(2, n, width), vmem(2, n, width), vmem(n, width), vmem(n, width)]
        + [vmem(2, n, width // 2)] * 3
        + [sems(2 * parts)] * 3 + [sems(parts)] * 2 + [sems(hops)] * 4,
        compiler_params=pltpu.CompilerParams(collective_id=1, has_side_effects=True, vmem_limit_bytes=LIMIT),
        cost_estimate=pl.CostEstimate(flops=0, bytes_accessed=2**26, transcendentals=0),
        name="reduce_all",
    )(x)


def sds(shape, dtype):
    return jax.ShapeDtypeStruct(shape, dtype)


def whole(shape):
    return pl.BlockSpec(shape, lambda *_: (0,) * len(shape), pipeline_mode=pl.Buffered(1))


def tables(start, count):
    half = HEAD_DIM // 2
    freqs = rope_base ** (-(jnp.arange(half, dtype=f32) * 2.0 / HEAD_DIM))
    positions = (start + jnp.arange(count, dtype=jnp.int32)).astype(f32)
    angles = positions[:, None] * freqs[None, :]
    cos, sin = jnp.cos(angles), jnp.sin(angles)
    none = jnp.zeros_like(sin)
    return (
        jnp.concatenate([cos] * 4, axis=-1),
        jnp.concatenate([-sin, none] * 2, axis=-1),
        jnp.concatenate([none, sin] * 2, axis=-1),
    )


def shards(tokens, norm_gain_attn, qkv_weight, attn_out_weight, norm_gain_mlp, mlp_in_weight, mlp_out_weight, grad_out):
    seqs, piece, width = tokens.shape
    rows = seqs * piece
    span = piece + 2 * WIN
    pairs = width // PAIR
    seq_size = lax.axis_size("seq")
    shares = lax.axis_size("fsdp")
    mlp_shapes = (mlp_in_weight.shape, attn_out_weight.shape, mlp_out_weight.shape)
    mlp_rows = sum(n * m // width for n, m in mlp_shapes)
    qkv_rows = padded_rows(3 * qkv_weight.shape[0] + 16, seq_size)
    forward = [(i, i + 1) for i in range(seq_size - 1)]
    backward = [(j, i) for i, j in forward]
    gather = lambda x: lax.all_gather(x, "fsdp", axis=0, tiled=True)
    gains = jnp.stack([norm_gain_attn, norm_gain_mlp])
    own_gains = gains.shape[1]
    gains = jnp.pad(gains, ((0, 30), (0, -own_gains % PAIR)))
    w_qkv, gains = gather_weights(qkv_weight, gains)
    gains = gains.reshape(shares, 32, -1)[:, :2, :own_gains].swapaxes(0, 1).reshape(2, width)
    w_attn = gather(attn_out_weight)
    w_in = gather(mlp_in_weight)
    w_out = gather(mlp_out_weight)
    gain_attn = gains[0:1].astype(f32)
    gain_mlp = gains[1:2].astype(f32)
    start = lax.axis_index("seq") * piece
    cos, low, high = tables(start - WIN, span)
    q_at = start + jnp.arange(piece, dtype=jnp.int32).reshape(-1, BLOCK)[:, None, :]
    k_at = (
        start - WIN
        + jnp.arange(piece // BLOCK, dtype=jnp.int32)[:, None, None] * BLOCK
        + jnp.arange(BLOCK + 2 * WIN, dtype=jnp.int32)[None, :, None]
    )
    inside = (jnp.abs(q_at - k_at) <= WIN) & (k_at >= 0) & (k_at < piece * seq_size)
    bias = jnp.tile(jnp.where(inside, 0.0, negative).astype(f32), (1, 1, 2))

    tile = 256
    per = piece // tile
    flat = lambda x: x.reshape(rows, x.shape[-1])
    row_spec = lambda w: pl.BlockSpec((tile, w), lambda i: (i, 0))
    table_spec = pl.BlockSpec((tile, PAIR), lambda i: (lax.rem(i, per), 0))
    params = lambda n: pltpu.CompilerParams(dimension_semantics=("arbitrary",) * n, vmem_limit_bytes=LIMIT)
    tok = flat(tokens)
    mid = slice(WIN, WIN + piece)
    def project(x, *rotary):
        count = x.shape[0]
        return pl.pallas_call(
            qkv_kernel,
            grid=(count // tile,),
            in_specs=[row_spec(width), whole((1, width)), whole(w_qkv.shape), table_spec, table_spec, table_spec],
            out_specs=[row_spec(width), row_spec(2 * width)],
            out_shape=[sds((count, width), bf16), sds((count, 2 * width), bf16)],
            compiler_params=params(1),
            cost_estimate=pl.CostEstimate(flops=6 * count * width * width, bytes_accessed=12 * count * width, transcendentals=0),
            name="qkv_forward",
        )(x, gain_attn, w_qkv, *rotary)

    borders = lambda x, n: jnp.concatenate([x[..., :WIN, :], x[..., n - WIN :, :]], axis=-2)
    _, kv_border = project(
        borders(tokens, piece).reshape(-1, width),
        *(jnp.tile(borders(t[mid], piece), (seqs, 1)) for t in (cos, low, high)),
    )
    kv_border = kv_border.reshape(seqs, 2 * WIN, 2 * width)
    left = lax.ppermute(kv_border[:, WIN:], "seq", forward)
    right = lax.ppermute(kv_border[:, :WIN], "seq", backward)
    q, kv = project(tok, cos[mid], low[mid], high[mid])
    q = q.reshape(seqs, piece, width)
    kv = kv.reshape(seqs, piece, 2 * width)

    def lanes(n, off=0):
        return pl.BlockSpec((1, n, PAIR), lambda s, p: (s, 0, p + off))

    kv_specs = [
        lanes(piece), lanes(piece, pairs), lanes(WIN), lanes(WIN, pairs), lanes(WIN), lanes(WIN, pairs),
    ]
    kv_args = (kv, kv, left, left, right, right)
    p_block = (1, 1, piece // BLOCK, BLOCK + 2 * WIN, 2 * BLOCK)
    p_spec = pl.BlockSpec(p_block, lambda s, p: (s, p, 0, 0, 0))
    p_shape = (seqs, pairs) + p_block[2:]
    ext = pltpu.VMEM((span, PAIR), bf16)
    unit_flops = 2 * seqs * HEADS * piece * (BLOCK + 2 * WIN) * HEAD_DIM
    p_bytes = 2 * math.prod(p_shape)
    attended, probs = pl.pallas_call(
        attend_kernel,
        grid=(seqs, pairs),
        in_specs=[lanes(piece)] + kv_specs + [whole(bias.shape)],
        out_specs=[lanes(piece), p_spec],
        out_shape=[sds((seqs, piece, width), bf16), sds(p_shape, bf16)],
        scratch_shapes=[ext, ext],
        compiler_params=params(2),
        cost_estimate=pl.CostEstimate(flops=8 * unit_flops, bytes_accessed=p_bytes + 8 * rows * width, transcendentals=p_bytes // 2),
        name="attend_forward",
    )(q, *kv_args, bias)

    wide = piece
    wide_spec = pl.BlockSpec((wide, width), lambda i: (i, 0))
    out, mg, ag, d_mlp, d_gain_mlp = pl.pallas_call(
        functools.partial(mlp_kernel, rows // wide),
        grid=(rows // wide,),
        in_specs=[wide_spec] * 3 + [whole((1, width)), whole(w_attn.shape), whole(w_in.shape), whole(w_out.shape)],
        out_specs=[wide_spec] * 3
        + [whole((shares, mlp_rows, width)), whole((1, width))],
        out_shape=[
            sds((rows, width), bf16), sds((rows, width), f32), sds((rows, width), bf16),
            sds((shares, mlp_rows, width), bf16), sds((1, width), f32),
        ],
        scratch_shapes=[
            pltpu.VMEM(w_attn.shape, f32), pltpu.VMEM(w_in.shape, f32), pltpu.VMEM(w_out.shape, f32),
            pltpu.VMEM((wide, 2 * FF), bf16), pltpu.VMEM((wide, FF), bf16),
        ],
        compiler_params=params(1),
        cost_estimate=pl.CostEstimate(flops=6 * rows * width * (width + 3 * FF), bytes_accessed=40 * 2**20, transcendentals=0),
        name="mlp_both_ways",
    )(tok, flat(attended), flat(grad_out), gain_mlp, w_attn, w_in, w_out)

    mlp_share = lax.psum_scatter(d_mlp, "fsdp", scatter_dimension=0, tiled=True)[0]

    table_full = pl.BlockSpec((span, PAIR), lambda p: (0, 0))
    edge_shape = sds((1, 2, WIN, width), bf16)
    own = sds((1, piece, width), bf16)
    total = pltpu.VMEM((span, PAIR), f32)
    ag = ag.reshape(seqs, piece, width)
    mg = mg.reshape(seqs, piece, width)

    def attend_back(s):
        def at(n, off=0):
            return pl.BlockSpec((1, n, PAIR), lambda p: (s, 0, p + off))

        here = pl.BlockSpec((1, piece, PAIR), lambda p: (0, 0, p))
        edge = pl.BlockSpec((1, 2, WIN, PAIR), lambda p: (0, 0, 0, p))
        return pl.pallas_call(
            attend_back_kernel,
            grid=(pairs,),
            in_specs=[at(piece), at(piece), at(piece, pairs), at(WIN), at(WIN, pairs), at(WIN), at(WIN, pairs)]
            + [pl.BlockSpec(p_block, lambda p: (s, p, 0, 0, 0)), at(piece)]
            + [table_full] * 3,
            out_specs=[here] * 3 + [edge, edge],
            out_shape=[own] * 3 + [edge_shape] * 2,
            scratch_shapes=[ext, ext, total, total],
            compiler_params=params(1),
            cost_estimate=pl.CostEstimate(flops=8 * unit_flops, bytes_accessed=p_bytes // 2 + 8 * rows * width, transcendentals=0),
            name="attend_backward",
        )(q, *kv_args, probs, ag, cos, low, high)

    one = pl.BlockSpec((1, piece, width), lambda i: (0, 0, 0))
    edge_in = pl.BlockSpec((1, 2, WIN, width), lambda i: (0, 0, 0, 0))

    def qkv_back(s, grads, before, tokens_grad):
        this = pl.BlockSpec((1, piece, width), lambda i: (s, 0, 0))
        last = s == seqs - 1
        prior = [] if before is None else list(before)
        to = (shares, qkv_rows, width) if last else w_qkv.shape
        kept = [] if tokens_grad is None else [tokens_grad]
        args = [tokens, mg, *grads, gain_attn, w_qkv, *prior, *kept]
        return pl.pallas_call(
            functools.partial(qkv_back_kernel, len(prior), len(kept), last),
            grid=(1,),
            in_specs=[this] * 2 + [one] * 3 + [edge_in] * 2 + [whole((1, width)), whole(w_qkv.shape)]
            + [whole(p.shape) for p in prior] + [pl.BlockSpec(memory_space=pl.ANY)] * len(kept),
            out_specs=[this, whole(to), whole((1, width))],
            out_shape=[sds(tokens.shape, f32), sds(to, bf16), sds((1, width), f32)],
            scratch_shapes=[pltpu.VMEM((piece, 3 * width), bf16)],
            input_output_aliases={len(args) - 1: 0} if kept else {},
            compiler_params=params(1),
            cost_estimate=pl.CostEstimate(flops=12 * piece * width * width, bytes_accessed=20 * piece * width, transcendentals=0),
            name="qkv_backward",
        )(*args)

    grads = []
    for s in range(seqs):
        dq, dk, dv, dl, dr = attend_back(s)
        grads.append((dq, dk, dv, lax.ppermute(dr, "seq", forward), lax.ppermute(dl, "seq", backward)))
    before = tokens_grad = None
    for s in range(seqs):
        tokens_grad, *before = qkv_back(s, grads[s], before, tokens_grad)
    d_wqkv, d_gain_attn = before

    gains_at = 3 * qkv_weight.shape[0]
    both = jnp.concatenate([d_gain_attn, d_gain_mlp]).astype(bf16)
    both = both.reshape(2, shares, width // shares).swapaxes(0, 1)
    both = jnp.pad(both, ((0, 0), (0, 0), (0, width - width // shares)))
    d_wqkv = lax.dynamic_update_slice(d_wqkv, both, (0, gains_at, 0))
    mlp_share, d_wqkv = lax.optimization_barrier((mlp_share, d_wqkv))
    mlp_sum = lax.psum(mlp_share, "seq")
    qkv_sum = reduce_all(d_wqkv, 4, seq_size)
    s_wqkv = unpack(qkv_sum, (qkv_weight.shape,))[0]
    s_gains = qkv_sum[gains_at : gains_at + 2, : width // shares].astype(f32)
    s_win, s_wo, s_wout = unpack(mlp_sum, mlp_shapes)
    return (
        out.reshape(seqs, piece, width),
        tokens_grad,
        s_gains[0],
        s_wqkv.astype(f32),
        s_wo.astype(f32),
        s_gains[1],
        s_win.astype(f32),
        s_wout.astype(f32),
    )


def solution(mesh):
    return jax.shard_map(
        shards,
        mesh=mesh,
        in_specs=(
            P("fsdp", "seq", None),
            P("fsdp"),
            P("fsdp", None),
            P("fsdp", None),
            P("fsdp"),
            P("fsdp", None),
            P("fsdp", None),
            P("fsdp", "seq", None),
        ),
        out_specs=(
            P("fsdp", "seq", None),
            P("fsdp", "seq", None),
            P("fsdp"),
            P("fsdp", None),
            P("fsdp", None),
            P("fsdp"),
            P("fsdp", None),
            P("fsdp", None),
        ),
        check_vma=False,
    )
```
